512 devices in a mesh: dom: 128 (over y, z, core), cuts: 4 (over x).
Axes of the slice: x: 4, y: 8, z: 8, core: 2. Of those that a mesh axis runs over, the one named last changes fastest.
Arguments:
- features: bfloat16 [196608, 128], P(('dom', 'cuts')), may hold values from -6 to 6
- weight_one: bfloat16 [128, 256], replicated, may hold values from -0.5 to 0.5
- bias_one: float32 [256], replicated, may hold values from -3 to 3
- weight_two: bfloat16 [256, 256], replicated, may hold values from -0.375 to 0.375
- bias_two: float32 [256], replicated, may hold values from -3 to 3
- hub_rows: int32 [128, 4, 16], P('dom', 'cuts'), may hold values from 0 to 383, as said below
- halo_rows: int32 [128, 4, 128, 16], P('dom', 'cuts'), may hold values from 0 to 383
- halo_count: int32 [128, 4, 128], P('dom', 'cuts'), may hold values from 0 to 16, as said below
- tile_target: int32 [128, 4, 16], P('dom', 'cuts'), may hold values from 0 to 11
- tile_source: int32 [128, 4, 16], P('dom', 'cuts'), may hold values from 0 to 34
- tile_count: int32 [128, 4], P('dom', 'cuts'), may hold values from 4 to 16, as said below
- tile_values: bfloat16 [128, 4, 16, 128, 128], P('dom', 'cuts'), may hold values from -0.25 to 0.25
Outputs:
- hidden_two: bfloat16 [196608, 256], P(('dom', 'cuts'))
The draws below stay inside these ranges and needn't reach their ends.
Inputs may be any that keep to these rules, and one draw needn't show every extreme that they name: `hub_rows`: the 16 rows of each slice are distinct. `halo_count`: A partition sends nothing to itself (count 0); some pair uses all 16 rows. `tile_count`: some slice uses all 16 tiles.
All inputs are finite; a program needn't handle non-finite values.
Results may differ from the reference program's by a relative error of at most 0.0054.
Values may be sent and summed in bfloat16 or wider, within the bound.
No kernel may reach another device: no remote copies, remote signals or barrier semaphores. Data moves between devices by JAX's collectives and lax.ppermute only.
A program may use at most 64 MiB of HBM per device.

```python
import jax
import jax.numpy as jnp
from jax import lax

F_IN = 128
HID = 256
BLOCK = 128
ROWS_DEV = 384
SLOT = 16
HUB = 16
TILE_CAP = 16
NODES = 196608
ROW_BLOCKS = 12
SRC_BLOCKS = 35
N_DOM = 128
N_CUTS = 4


def draw_hub_rows(key, part):
    key = jax.random.fold_in(key, 11)
    keys = jax.random.split(key, N_DOM * N_CUTS)
    rows = jax.vmap(lambda single: jax.random.permutation(single, ROWS_DEV)[:HUB])(keys)
    return rows.reshape(N_DOM, N_CUTS, HUB).astype(jnp.int32)


def draw_halo_count(key, part):
    key = jax.random.fold_in(key, 23)
    first, second, third, fourth = jax.random.split(key, 4)
    counts = jax.random.randint(first, (N_DOM, N_CUTS, N_DOM), 0, SLOT + 1)
    sender = jnp.arange(N_DOM, dtype=jnp.int32)[:, None, None]
    target = jnp.arange(N_DOM, dtype=jnp.int32)[None, None, :]
    counts = jnp.where(sender == target, 0, counts)
    pick_part = jax.random.randint(second, (), 0, N_DOM)
    pick_cut = jax.random.randint(third, (), 0, N_CUTS)
    pick_dest = (pick_part + 1 + jax.random.randint(fourth, (), 0, max(N_DOM - 1, 1))) % N_DOM
    counts = counts.at[pick_part, pick_cut, pick_dest].set(SLOT)
    return counts.astype(jnp.int32)


def draw_tile_count(key, part):
    key = jax.random.fold_in(key, 37)
    first, second = jax.random.split(key)
    counts = jax.random.randint(first, (N_DOM * N_CUTS,), TILE_CAP // 4, TILE_CAP + 1)
    full_one = jax.random.randint(second, (), 0, N_DOM * N_CUTS)
    counts = counts.at[full_one].set(TILE_CAP)
    return counts.reshape(N_DOM, N_CUTS).astype(jnp.int32)


def touch_ends(result, stream_key, least, high):
    index_at = [jax.random.randint(jax.random.fold_in(stream_key, axis), (), 0, length) for axis, length in enumerate(result.shape)]
    longest = result.shape.index(max(result.shape))
    beside = index_at[:longest] + [(index_at[longest] + 1) % result.shape[longest]] + index_at[longest + 1:]
    return result.at[tuple(index_at)].set(least).at[tuple(beside)].set(high)


def levels(key, dims, shards, low, high):
    level = 1.0
    for position, shards_of in shards:
        steps = jax.random.uniform(jax.random.fold_in(jax.random.fold_in(key, 6), position), (shards_of,), jnp.float32, low / len(shards), high / len(shards))
        level = level * jnp.repeat(jnp.exp(steps), dims[position] // shards_of).reshape((-1,) + (1,) * (len(dims) - 1 - position))
    return level


def noise(key, dims, spread, bound, cuts=(), held_as=jnp.bfloat16):
    array = jax.random.normal(key, dims, jnp.float32) * spread
    if len(cuts) > 0:
        array = levels(key, dims, cuts, -0.22, 0.18) * array
    return jnp.clip(array, min=-bound, max=bound).astype(held_as)


def setup_inputs(seed: int = 0) -> dict:
    key_list = jax.random.split(jax.random.key(seed), 13)
    return {
        "features": noise(key_list[0], (NODES, F_IN), 1.0, 6.0, ((0, 512),)),
        "weight_one": noise(key_list[1], (F_IN, HID), F_IN ** -0.5, 0.5),
        "bias_one": noise(key_list[2], (HID,), 0.5, 3.0, (), jnp.float32),
        "weight_two": noise(key_list[3], (HID, HID), HID ** -0.5, 0.375),
        "bias_two": noise(key_list[4], (HID,), 0.5, 3.0, (), jnp.float32),
        "hub_rows": draw_hub_rows(jax.random.fold_in(key_list[12], 71), 0),
        "halo_rows": touch_ends(jax.random.randint(key_list[6], (N_DOM, N_CUTS, N_DOM, SLOT), 0, ROWS_DEV), jax.random.fold_in(key_list[6], 1), 0, ROWS_DEV - 1).astype(jnp.int32),
        "halo_count": draw_halo_count(jax.random.fold_in(key_list[12], 71), 0),
        "tile_target": touch_ends(jax.random.randint(key_list[8], (N_DOM, N_CUTS, TILE_CAP), 0, ROW_BLOCKS), jax.random.fold_in(key_list[8], 1), 0, ROW_BLOCKS - 1).astype(jnp.int32),
        "tile_source": touch_ends(jax.random.randint(key_list[9], (N_DOM, N_CUTS, TILE_CAP), 0, SRC_BLOCKS), jax.random.fold_in(key_list[9], 1), 0, SRC_BLOCKS - 1).astype(jnp.int32),
        "tile_count": draw_tile_count(jax.random.fold_in(key_list[12], 71), 0),
        "tile_values": noise(key_list[11], (N_DOM, N_CUTS, TILE_CAP, BLOCK, BLOCK), (TILE_CAP * 32) ** -0.5, 0.25, ((0, 128), (1, 4))),
    }


def aggregate_all(table, halo_rows, halo_count, hub_rows, tile_target, tile_source, tile_count, tile_values, bias):
    slices = table.reshape(N_DOM, N_CUTS, ROWS_DEV, HID)
    hubs = jnp.take_along_axis(slices, hub_rows.astype(jnp.int32)[..., None], axis=2)
    hub_source = hubs.transpose(1, 0, 2, 3).reshape(N_CUTS, N_DOM * HUB, HID)
    slot_ids = jnp.arange(SLOT, dtype=jnp.int32)
    tile_ids = jnp.arange(TILE_CAP, dtype=jnp.int32)

    def one_part(part_id):
        picks = halo_rows[:, :, part_id, :].astype(jnp.int32)
        halo = jnp.take_along_axis(slices, picks[..., None], axis=2)
        live_slots = slot_ids[None, None, :] < halo_count[:, :, part_id][..., None]
        halo = jnp.where(live_slots[..., None], halo, jnp.zeros((), table.dtype))
        halo_source = halo.transpose(1, 0, 2, 3).reshape(N_CUTS, N_DOM * SLOT, HID)
        own_rows = lax.dynamic_index_in_dim(slices, part_id, 0, keepdims=False)
        sources = jnp.concatenate([own_rows, halo_source, hub_source], axis=1)
        sources = sources.reshape(N_CUTS, SRC_BLOCKS, BLOCK, HID)
        columns = tile_source[part_id].astype(jnp.int32)
        picked = jnp.take_along_axis(sources, columns[:, :, None, None], axis=1)
        tiles = tile_values[part_id].astype(jnp.float32)
        products = jnp.einsum('ctij,ctjf->ctif', tiles, picked.astype(jnp.float32))
        valid = tile_ids[None, :] < tile_count[part_id][:, None]
        products = jnp.where(valid[..., None, None], products, jnp.zeros((), jnp.float32))
        summed = jax.ops.segment_sum(products.reshape(N_CUTS * TILE_CAP, BLOCK, HID),
                                     tile_target[part_id].reshape(-1).astype(jnp.int32),
                                     num_segments=ROW_BLOCKS)
        return summed.reshape(ROW_BLOCKS * BLOCK, HID)

    totals = lax.map(one_part, jnp.arange(N_DOM, dtype=jnp.int32)).reshape(NODES, HID)
    return jax.nn.relu(totals + bias[None, :]).astype(jnp.bfloat16)


def reference(features, weight_one, bias_one, weight_two, bias_two, hub_rows, halo_rows, halo_count, tile_target, tile_source, tile_count, tile_values):
    proj_one = jnp.dot(features, weight_one, preferred_element_type=jnp.float32).astype(jnp.bfloat16)
    hidden_one = aggregate_all(proj_one, halo_rows, halo_count, hub_rows, tile_target, tile_source, tile_count, tile_values, bias_one)
    proj_two = jnp.dot(hidden_one, weight_two, preferred_element_type=jnp.float32).astype(jnp.bfloat16)
    return aggregate_all(proj_two, halo_rows, halo_count, hub_rows, tile_target, tile_source, tile_count, tile_values, bias_two)
```

```python
import jax
import jax.numpy as jnp
from jax import lax
from jax.experimental import pallas as pl
from jax.experimental.pallas import tpu as pltpu
from jax.sharding import PartitionSpec as P

ROWS = 384
SLOT = 16
HUB = 16
BLOCK = 128
CHUNK = 16
VMEM = pltpu.VMEM
SMEM = pltpu.SMEM
F32 = jnp.float32
BF16 = jnp.bfloat16


def spec(space):
    return pl.BlockSpec(memory_space=space)


def call(body, out_shape, spaces, scratch=()):
    return pl.pallas_call(
        body,
        out_shape=out_shape,
        in_specs=[spec(s) for s in spaces],
        out_specs=jax.tree.map(lambda _: spec(VMEM), out_shape),
        scratch_shapes=list(scratch),
        compiler_params=pltpu.CompilerParams(vmem_limit_bytes=40 * 1024 * 1024),
    )


def column(row, size):
    here = lax.broadcasted_iota(jnp.int32, (size, size), 0)
    there = lax.broadcasted_iota(jnp.int32, (size, size), 1)
    return jnp.sum(jnp.where(here == there, row, 0), axis=1, keepdims=True)


def one_hot(picks, depth):
    places = lax.broadcasted_iota(jnp.int32, (picks.shape[0], depth), 1)
    return jnp.where(picks == places, 1.0, 0.0).astype(BF16)


def fill_outgoing(table, halo_rows, halo_count, hub_rows, out):
    parts, slots = halo_rows.shape
    counts = column(halo_count[...], parts)
    slot = lax.broadcasted_iota(jnp.int32, (parts, slots), 1)
    picks = jnp.where(slot < counts, halo_rows[...], -1)
    hubs = jnp.dot(
        one_hot(column(hub_rows[...], HUB), ROWS), table, preferred_element_type=F32
    ).astype(BF16)
    for first in range(0, parts, CHUNK):
        some = picks[first : first + CHUNK]
        wide = jnp.broadcast_to(some[:, :, None], (CHUNK, slots, ROWS)).reshape(
            CHUNK * slots, ROWS
        )
        places = lax.broadcasted_iota(jnp.int32, (CHUNK * slots, ROWS), 1)
        chosen = jnp.where(wide == places, 1.0, 0.0).astype(BF16)
        rows = jnp.dot(chosen, table, preferred_element_type=F32).astype(BF16)
        out[first : first + CHUNK, :slots] = rows.reshape(CHUNK, slots, -1)
        out[first : first + CHUNK, slots:] = jnp.broadcast_to(
            hubs[None], (CHUNK,) + hubs.shape
        )


def pack_body(table, halo_rows, halo_count, hub_rows, out):
    fill_outgoing(table[...], halo_rows, halo_count, hub_rows, out)


def pack(table, halo_rows, halo_count, hub_rows):
    parts = halo_rows.shape[0]
    return call(
        pack_body,
        jax.ShapeDtypeStruct((parts, SLOT + HUB, table.shape[1]), BF16),
        [VMEM] * 4,
    )(table, halo_rows, halo_count, hub_rows)


def sum_body(targets, sources, count, own, incoming, tiles, out, mine, total):
    total[...] = jnp.zeros_like(total)
    capacity = tiles.shape[0]
    group = BLOCK // SLOT
    groups = incoming.shape[0] // group
    own_blocks = ROWS // BLOCK
    width = own.shape[1]
    used = count[0]
    for i in range(capacity):
        col = sources[i]
        here = jnp.minimum(col, own_blocks - 1)
        local_rows = own[pl.ds(pl.multiple_of(here * BLOCK, BLOCK), BLOCK), :]
        away = jnp.maximum(col - own_blocks, 0)
        hub = jnp.where(away >= groups, 1, 0)
        first = pl.multiple_of((away - hub * groups) * group, group)
        remote_rows = incoming[
            pl.ds(first, group), pl.ds(pl.multiple_of(hub * SLOT, SLOT), SLOT), :
        ].reshape(BLOCK, width)
        rows = jnp.where(col < own_blocks, local_rows, remote_rows)
        term = jnp.dot(tiles[i], rows, preferred_element_type=F32)
        row = targets[i]
        total[row] = total[row] + jnp.where(i < used, term, 0.0)
    chunk = ROWS // BLOCK
    cut = lax.axis_index("cuts")
    mine[...] = total[pl.ds(cut * chunk, chunk)].reshape(ROWS, width)
    out[...] = total[...].astype(BF16).reshape(out.shape)


def tile_sums(own, incoming, tile_target, tile_source, tile_count, tiles, cuts):
    width = own.shape[1]
    return call(
        sum_body,
        (
            jax.ShapeDtypeStruct((cuts, ROWS, width), BF16),
            jax.ShapeDtypeStruct((ROWS, width), F32),
        ),
        [SMEM] * 3 + [VMEM] * 3,
        [pltpu.VMEM((cuts * ROWS // BLOCK, BLOCK, width), F32)],
    )(tile_target, tile_source, tile_count, own, incoming, tiles)


def over_cuts(parts, mine):
    cut = lax.axis_index("cuts")
    total = mine[...]
    for k in range(parts.shape[0]):
        total = total + jnp.where(cut == k, 0.0, parts[k].astype(F32))
    return total


def middle_body(
    parts, mine, w_one, b_one, w_two, halo_rows, halo_count, hub_rows, table, out
):
    total = over_cuts(parts, mine)
    high = total.astype(BF16)
    low = (total - high.astype(F32)).astype(BF16)
    hidden = jnp.dot(high, w_one[...], preferred_element_type=F32) + jnp.dot(
        low, w_one[...], preferred_element_type=F32
    )
    hidden = jnp.maximum(hidden + b_one[...], 0.0).astype(BF16)
    projected = jnp.dot(hidden, w_two[...], preferred_element_type=F32).astype(BF16)
    table[...] = projected
    fill_outgoing(projected, halo_rows, halo_count, hub_rows, out)


def middle(parts, mine, w_one, b_one, w_two, halo_rows, halo_count, hub_rows):
    width = w_two.shape[1]
    return call(
        middle_body,
        (
            jax.ShapeDtypeStruct((ROWS, width), BF16),
            jax.ShapeDtypeStruct((halo_rows.shape[0], SLOT + HUB, width), BF16),
        ),
        [VMEM] * 8,
    )(parts, mine, w_one, b_one, w_two, halo_rows, halo_count, hub_rows)


def last_body(parts, mine, bias, out):
    out[...] = jnp.maximum(over_cuts(parts, mine) + bias[...], 0.0).astype(BF16)


def swap(rows, axis):
    return lax.all_to_all(rows, axis, split_axis=0, concat_axis=0, tiled=True)


def local(
    features,
    weight_one,
    bias_one,
    weight_two,
    bias_two,
    hub_rows,
    halo_rows,
    halo_count,
    tile_target,
    tile_source,
    tile_count,
    tile_values,
):
    cuts = lax.axis_size("cuts")
    halo_rows = halo_rows.reshape(halo_rows.shape[2:])
    halo_count = halo_count.reshape(1, -1)
    hub_rows = hub_rows.reshape(1, -1)
    tiles = tile_values.reshape(tile_values.shape[2:])
    plan = (tile_target.reshape(-1), tile_source.reshape(-1), tile_count.reshape(-1))

    incoming = swap(pack(features, halo_rows, halo_count, hub_rows), "dom")
    parts, mine = tile_sums(features, incoming, *plan, tiles, cuts)
    table, outgoing = middle(
        swap(parts, "cuts"),
        mine,
        weight_one,
        bias_one.reshape(1, -1),
        weight_two,
        halo_rows,
        halo_count,
        hub_rows,
    )
    incoming = swap(outgoing, "dom")
    parts, mine = tile_sums(table, incoming, *plan, tiles, cuts)
    return call(
        last_body, jax.ShapeDtypeStruct(table.shape, BF16), [VMEM] * 3
    )(swap(parts, "cuts"), mine, bias_two.reshape(1, -1))


def solution(mesh):
    return jax.shard_map(
        local,
        mesh=mesh,
        in_specs=(
            P(("dom", "cuts"), None),
            P(),
            P(),
            P(),
            P(),
            P("dom", "cuts", None),
            P("dom", "cuts", None, None),
            P("dom", "cuts", None),
            P("dom", "cuts", None),
            P("dom", "cuts", None),
            P("dom", "cuts"),
            P("dom", "cuts", None, None, None),
        ),
        out_specs=P(("dom", "cuts"), None),
        check_vma=False,
    )
```

```python
import jax
import jax.numpy as jnp
from jax import lax
from jax.experimental import pallas as pl
from jax.experimental.pallas import tpu as pltpu
from jax.sharding import PartitionSpec as P

ROWS = 384
SLOT = 16
HUB = 16
BLOCK = 128
CHUNK = 16
DEAD = 2.0**100
DEAD_LIMIT = 2.0**50
VMEM = pltpu.VMEM
SMEM = pltpu.SMEM
F32 = jnp.float32
BF16 = jnp.bfloat16


def spec(space):
    return pl.BlockSpec(memory_space=space)


def call(body, out_shape, spaces, scratch=()):
    return pl.pallas_call(
        body,
        out_shape=out_shape,
        in_specs=[spec(s) for s in spaces],
        out_specs=jax.tree.map(lambda _: spec(VMEM), out_shape),
        scratch_shapes=list(scratch),
        compiler_params=pltpu.CompilerParams(vmem_limit_bytes=40 * 1024 * 1024),
    )


def column(row, size):
    here = lax.broadcasted_iota(jnp.int32, (size, size), 0)
    there = lax.broadcasted_iota(jnp.int32, (size, size), 1)
    return jnp.sum(jnp.where(here == there, row, 0), axis=1, keepdims=True)


def one_hot(picks, depth):
    places = lax.broadcasted_iota(jnp.int32, (picks.shape[0], depth), 1)
    return jnp.where(picks == places, 1.0, 0.0).astype(BF16)


def fill_outgoing(table, halo_rows, halo_count, hub_rows, out, dead):
    parts, slots = halo_rows.shape
    width = table.shape[1]
    counts = column(halo_count[...], parts)
    slot = lax.broadcasted_iota(jnp.int32, (parts, slots), 1)
    picks = jnp.where(slot < counts, halo_rows[...], -1)
    hubs = jnp.dot(
        one_hot(column(hub_rows[...], HUB), ROWS), table, preferred_element_type=F32
    ).astype(BF16)
    for first in range(0, parts, CHUNK):
        some = picks[first : first + CHUNK]
        wide = jnp.broadcast_to(some[:, :, None], (CHUNK, slots, ROWS)).reshape(
            CHUNK * slots, ROWS
        )
        places = lax.broadcasted_iota(jnp.int32, (CHUNK * slots, ROWS), 1)
        chosen = jnp.where(wide == places, 1.0, 0.0).astype(BF16)
        rows = jnp.dot(chosen, table, preferred_element_type=F32)
        if dead != 0.0:
            rows = jnp.where(wide[:, :width] < 0, dead, rows)
        out[first : first + CHUNK, :slots] = rows.astype(BF16).reshape(
            CHUNK, slots, width
        )
        out[first : first + CHUNK, slots:] = jnp.broadcast_to(
            hubs[None], (CHUNK,) + hubs.shape
        )


def pack_body(table, halo_rows, halo_count, hub_rows, out):
    fill_outgoing(table[...], halo_rows, halo_count, hub_rows, out, 0.0)


def pack(table, halo_rows, halo_count, hub_rows):
    parts = halo_rows.shape[0]
    return call(
        pack_body,
        jax.ShapeDtypeStruct((parts, SLOT + HUB, table.shape[1]), BF16),
        [VMEM] * 4,
    )(table, halo_rows, halo_count, hub_rows)


def sum_body(targets, sources, count, own, incoming, tiles, *rest):
    *layer, out, mine, total = rest
    total[...] = jnp.zeros_like(total)
    capacity = tiles.shape[0]
    group = BLOCK // SLOT
    groups = incoming.shape[0] // group
    own_blocks = ROWS // BLOCK
    used = count[0]
    for i in range(capacity):
        col = sources[i]
        here = jnp.minimum(col, own_blocks - 1)
        local_rows = own[pl.ds(pl.multiple_of(here * BLOCK, BLOCK), BLOCK), :]
        away = jnp.maximum(col - own_blocks, 0)
        hub = jnp.where(away >= groups, 1, 0)
        first = pl.multiple_of((away - hub * groups) * group, group)
        remote_rows = incoming[
            pl.ds(first, group), pl.ds(pl.multiple_of(hub * SLOT, SLOT), SLOT), :
        ].reshape(BLOCK, own.shape[1])
        rows = jnp.where(col < own_blocks, local_rows, remote_rows)
        if layer:
            weight, bias = layer
            hidden = jnp.dot(rows, weight[...], preferred_element_type=F32)
            hidden = jnp.maximum(hidden + bias[...], 0.0)
            live = rows.astype(F32) < DEAD_LIMIT
            live = jnp.concatenate([live] * (hidden.shape[1] // live.shape[1]), axis=1)
            rows = jnp.where(live, hidden, 0.0).astype(BF16)
        term = jnp.dot(tiles[i], rows, preferred_element_type=F32)
        row = targets[i]
        total[row] = total[row] + jnp.where(i < used, term, 0.0)
    chunk = ROWS // BLOCK
    cut = lax.axis_index("cuts")
    mine[...] = total[pl.ds(cut * chunk, chunk)].reshape(mine.shape)
    out[...] = total[...].astype(BF16).reshape(out.shape)


def tile_sums(own, incoming, tile_target, tile_source, tile_count, tiles, cuts, *layer):
    width = layer[0].shape[1] if layer else own.shape[1]
    return call(
        sum_body,
        (
            jax.ShapeDtypeStruct((cuts, ROWS, width), BF16),
            jax.ShapeDtypeStruct((ROWS, width), F32),
        ),
        [SMEM] * 3 + [VMEM] * (3 + len(layer)),
        [pltpu.VMEM((cuts * ROWS // BLOCK, BLOCK, width), F32)],
    )(tile_target, tile_source, tile_count, own, incoming, tiles, *layer)


def over_cuts(parts, mine):
    cut = lax.axis_index("cuts")
    total = mine[...]
    for k in range(parts.shape[0]):
        total = total + jnp.where(cut == k, 0.0, parts[k].astype(F32))
    return total


def middle_body(parts, mine, halo_rows, halo_count, hub_rows, table, out):
    rows = over_cuts(parts, mine).astype(BF16)
    table[...] = rows
    fill_outgoing(rows, halo_rows, halo_count, hub_rows, out, DEAD)


def middle(parts, mine, halo_rows, halo_count, hub_rows):
    width = mine.shape[1]
    return call(
        middle_body,
        (
            jax.ShapeDtypeStruct((ROWS, width), BF16),
            jax.ShapeDtypeStruct((halo_rows.shape[0], SLOT + HUB, width), BF16),
        ),
        [VMEM] * 5,
    )(parts, mine, halo_rows, halo_count, hub_rows)


def last_body(parts, mine, weight, bias, out):
    total = over_cuts(parts, mine)
    high = total.astype(BF16)
    low = (total - high.astype(F32)).astype(BF16)
    hidden = jnp.dot(high, weight[...], preferred_element_type=F32) + jnp.dot(
        low, weight[...], preferred_element_type=F32
    )
    out[...] = jnp.maximum(hidden + bias[...], 0.0).astype(BF16)


def swap(rows, axis):
    return lax.all_to_all(rows, axis, split_axis=0, concat_axis=0, tiled=True)


def local(
    features,
    weight_one,
    bias_one,
    weight_two,
    bias_two,
    hub_rows,
    halo_rows,
    halo_count,
    tile_target,
    tile_source,
    tile_count,
    tile_values,
):
    cuts = lax.axis_size("cuts")
    halo_rows = halo_rows.reshape(halo_rows.shape[2:])
    halo_count = halo_count.reshape(1, -1)
    hub_rows = hub_rows.reshape(1, -1)
    tiles = tile_values.reshape(tile_values.shape[2:])
    plan = (tile_target.reshape(-1), tile_source.reshape(-1), tile_count.reshape(-1))

    incoming = swap(pack(features, halo_rows, halo_count, hub_rows), "dom")
    parts, mine = tile_sums(features, incoming, *plan, tiles, cuts)
    table, outgoing = middle(
        swap(parts, "cuts"), mine, halo_rows, halo_count, hub_rows
    )
    incoming = swap(outgoing, "dom")
    parts, mine = tile_sums(
        table, incoming, *plan, tiles, cuts, weight_one, bias_one.reshape(1, -1)
    )
    return call(
        last_body,
        jax.ShapeDtypeStruct((ROWS, weight_two.shape[1]), BF16),
        [VMEM] * 4,
    )(swap(parts, "cuts"), mine, weight_two, bias_two.reshape(1, -1))


def solution(mesh):
    return jax.shard_map(
        local,
        mesh=mesh,
        in_specs=(
            P(("dom", "cuts"), None),
            P(),
            P(),
            P(),
            P(),
            P("dom", "cuts", None),
            P("dom", "cuts", None, None),
            P("dom", "cuts", None),
            P("dom", "cuts", None),
            P("dom", "cuts", None),
            P("dom", "cuts"),
            P("dom", "cuts", None, None, None),
        ),
        out_specs=P(("dom", "cuts"), None),
        check_vma=False,
    )
```

```python
import jax
import jax.numpy as jnp
from jax import lax
from jax.experimental import pallas as pl
from jax.experimental.pallas import tpu as pltpu
from jax.sharding import PartitionSpec as P

ROWS = 384
SLOT = 16
HUB = 16
BLOCK = 128
CHUNK = 16
CORES = 2
DEAD = 2.0**100
DEAD_LIMIT = 2.0**50
VMEM = pltpu.VMEM
SMEM = pltpu.SMEM
F32 = jnp.float32
BF16 = jnp.bfloat16


def spec(space):
    return pl.BlockSpec(memory_space=space)


LIMIT = 40 * 1024 * 1024


def call(body, out_shape, spaces, scratch=()):
    return pl.pallas_call(
        body,
        out_shape=out_shape,
        in_specs=[spec(s) for s in spaces],
        out_specs=jax.tree.map(lambda _: spec(VMEM), out_shape),
        scratch_shapes=list(scratch),
        compiler_params=pltpu.CompilerParams(vmem_limit_bytes=LIMIT),
    )


def column(row, size):
    here = lax.broadcasted_iota(jnp.int32, (size, size), 0)
    there = lax.broadcasted_iota(jnp.int32, (size, size), 1)
    return jnp.sum(jnp.where(here == there, row, 0), axis=1, keepdims=True)


def one_hot(picks):
    places = lax.broadcasted_iota(jnp.int32, picks.shape, 1)
    return jnp.where(picks == places, 1.0, 0.0).astype(BF16)


def fill_outgoing(table, picks, hub_picks, out, dead):
    parts, slots = picks.shape
    width = table.shape[1]
    hubs = jnp.dot(one_hot(hub_picks), table, preferred_element_type=F32).astype(BF16)
    for first in range(0, parts, CHUNK):
        some = picks[first : first + CHUNK]
        wide = jnp.broadcast_to(some[:, :, None], (CHUNK, slots, ROWS)).reshape(
            CHUNK * slots, ROWS
        )
        rows = jnp.dot(one_hot(wide), table, preferred_element_type=F32)
        if dead != 0.0:
            rows = jnp.where(wide[:, :width] < 0, dead, rows)
        chips = pl.ds(first // CORES, CHUNK // CORES)
        out[chips, : CORES * slots] = rows.astype(BF16).reshape(
            CHUNK // CORES, CORES * slots, width
        )
        out[chips, CORES * slots :] = jnp.broadcast_to(
            hubs[None], (CHUNK // CORES,) + hubs.shape
        )


def pack_body(*refs):
    count = (len(refs) - 5) // 2
    sources, (out, picks_out, hubs_out, plan_out) = refs[:count], refs[count : count + 4]
    kept, sems = refs[count + 4 : -1], refs[-1]
    copies = [
        pltpu.make_async_copy(source, place, sems.at[i])
        for i, (source, place) in enumerate(zip(sources, kept, strict=True))
    ]
    for copy in copies:
        copy.start()
    for copy in copies:
        copy.wait()
    targets, columns, used, halo_rows, halo_count, hub_rows, table = kept[-7:]
    pieces = [targets[...], columns[...], used[...]]
    spare = plan_out.shape[1] - sum(piece.shape[1] for piece in pieces)
    plan_out[...] = jnp.concatenate(
        [*pieces, jnp.zeros((1, spare), jnp.int32)], axis=1
    )
    slots, parts = halo_rows.shape
    slot = lax.broadcasted_iota(jnp.int32, (slots, parts), 0)
    picks = jnp.where(slot < halo_count[...], halo_rows[...], -1).T
    hub_picks = jnp.broadcast_to(column(hub_rows[...], HUB), (HUB, ROWS))
    picks_out[...] = picks
    hubs_out[...] = hub_picks
    fill_outgoing(table[...], picks, hub_picks, out, 0.0)


def pack(handed, *operands):
    slots, parts = operands[-4].shape
    table = operands[-1]
    return pl.pallas_call(
        pack_body,
        out_shape=(
            jax.ShapeDtypeStruct((parts // CORES, CORES * SLOT + HUB, table.shape[1]), BF16),
            jax.ShapeDtypeStruct((parts, slots), jnp.int32),
            jax.ShapeDtypeStruct((HUB, ROWS), jnp.int32),
            jax.ShapeDtypeStruct((1, 128), jnp.int32),
            *(jax.ShapeDtypeStruct(x.shape, x.dtype) for x in handed),
        ),
        in_specs=[spec(pltpu.HBM)] * (len(handed) + len(operands)),
        out_specs=(spec(VMEM),) * (4 + len(handed)),
        scratch_shapes=[
            *(pltpu.VMEM(x.shape, x.dtype) for x in operands),
            pltpu.SemaphoreType.DMA((len(handed) + len(operands),)),
        ],
        compiler_params=pltpu.CompilerParams(vmem_limit_bytes=LIMIT),
    )(*handed, *operands)


def sum_body(plan, own, received, passed, tiles, *rest):
    *layer, out, mine, total = rest
    total[...] = jnp.zeros_like(total)
    capacity = tiles.shape[0]
    group = BLOCK // (CORES * SLOT)
    groups = received.shape[0] // group
    core = lax.rem(lax.axis_index("dom"), CORES)
    own_blocks = ROWS // BLOCK
    used = plan[2 * capacity]
    for i in range(capacity):
        col = plan[capacity + i]
        here = jnp.minimum(col, own_blocks - 1)
        local_rows = own[pl.ds(pl.multiple_of(here * BLOCK, BLOCK), BLOCK), :]
        away = jnp.maximum(col - own_blocks, 0)
        hub = jnp.where(away >= groups, 1, 0)
        first = pl.multiple_of((away - hub * groups) * group, group)
        start = pl.multiple_of(jnp.where(hub == 1, CORES * SLOT, core * SLOT), SLOT)
        same = received[pl.ds(first, group), pl.ds(start, SLOT), :]
        other = passed[pl.ds(first, group), pl.ds(start, SLOT), :]
        remote_rows = jnp.stack(
            [jnp.where(core == 0, same, other), jnp.where(core == 0, other, same)],
            axis=1,
        ).reshape(BLOCK, own.shape[1])
        rows = jnp.where(col < own_blocks, local_rows, remote_rows)
        if layer:
            weight, bias = layer
            hidden = jnp.dot(rows, weight[...], preferred_element_type=F32)
            hidden = jnp.maximum(hidden + bias[...], 0.0)
            live = rows.astype(F32) < DEAD_LIMIT
            live = jnp.concatenate([live] * (hidden.shape[1] // live.shape[1]), axis=1)
            rows = jnp.where(live, hidden, 0.0).astype(BF16)
        term = jnp.dot(tiles[i], rows, preferred_element_type=F32)
        row = plan[i]
        total[row] = total[row] + jnp.where(i < used, term, 0.0)
    chunk = ROWS // BLOCK
    cut = lax.axis_index("cuts")
    mine[...] = total[pl.ds(cut * chunk, chunk)].reshape(mine.shape)
    out[...] = total[...].astype(BF16).reshape(out.shape)


def tile_sums(own, received, passed, plan, tiles, cuts, *layer):
    width = layer[0].shape[1] if layer else own.shape[1]
    return call(
        sum_body,
        (
            jax.ShapeDtypeStruct((cuts, ROWS, width), BF16),
            jax.ShapeDtypeStruct((ROWS, width), F32),
        ),
        [SMEM] + [VMEM] * (4 + len(layer)),
        [pltpu.VMEM((cuts * ROWS // BLOCK, BLOCK, width), F32)],
    )(plan, own, received, passed, tiles, *layer)


def over_cuts(parts, mine):
    cut = lax.axis_index("cuts")
    total = mine[...]
    for k in range(parts.shape[0]):
        total = total + jnp.where(cut == k, 0.0, parts[k].astype(F32))
    return total


def middle_body(parts, mine, picks, hub_picks, table, out):
    rows = over_cuts(parts, mine).astype(BF16)
    table[...] = rows
    fill_outgoing(rows, picks[...], hub_picks[...], out, DEAD)


def middle(parts, mine, picks, hub_picks):
    width = mine.shape[1]
    return call(
        middle_body,
        (
            jax.ShapeDtypeStruct((ROWS, width), BF16),
            jax.ShapeDtypeStruct((picks.shape[0] // CORES, CORES * SLOT + HUB, width), BF16),
        ),
        [VMEM] * 4,
    )(parts, mine, picks, hub_picks)


def last_body(parts, mine, weight, bias, out):
    total = over_cuts(parts, mine)
    high = total.astype(BF16)
    low = (total - high.astype(F32)).astype(BF16)
    hidden = jnp.dot(high, weight[...], preferred_element_type=F32) + jnp.dot(
        low, weight[...], preferred_element_type=F32
    )
    out[...] = jnp.maximum(hidden + bias[...], 0.0).astype(BF16)


def swap(rows, axis):
    return lax.all_to_all(rows, axis, split_axis=0, concat_axis=0, tiled=True)


def exchange(rows):
    size = lax.axis_size("dom")
    alike = [list(range(core, size, CORES)) for core in range(CORES)]
    received = lax.all_to_all(
        rows, "dom", split_axis=0, concat_axis=0, tiled=True, axis_index_groups=alike
    )
    return received, lax.ppermute(received, "dom", [(i, i ^ 1) for i in range(size)])


def local(
    features,
    weight_one,
    bias_one,
    weight_two,
    bias_two,
    hub_rows,
    halo_rows,
    halo_count,
    tile_target,
    tile_source,
    tile_count,
    tile_values,
):
    cuts = lax.axis_size("cuts")
    halo_rows = halo_rows.reshape(halo_rows.shape[2:]).T
    tiles = tile_values.reshape(tile_values.shape[2:])
    row = lambda x: x.reshape(1, -1)
    outgoing, picks, hub_picks, plan, bias_one, bias_two = pack(
        (row(bias_one), row(bias_two)),
        row(tile_target),
        row(tile_source),
        row(tile_count),
        halo_rows,
        row(halo_count),
        row(hub_rows),
        features,
    )
    plan = plan.reshape(-1)
    parts, mine = tile_sums(features, *exchange(outgoing), plan, tiles, cuts)
    table, outgoing = middle(swap(parts, "cuts"), mine, picks, hub_picks)
    parts, mine = tile_sums(
        table, *exchange(outgoing), plan, tiles, cuts, weight_one, bias_one
    )
    return call(
        last_body,
        jax.ShapeDtypeStruct((ROWS, weight_two.shape[1]), BF16),
        [VMEM] * 4,
    )(swap(parts, "cuts"), mine, weight_two, bias_two)


def solution(mesh):
    return jax.shard_map(
        local,
        mesh=mesh,
        in_specs=(
            P(("dom", "cuts"), None),
            P(),
            P(),
            P(),
            P(),
            P("dom", "cuts", None),
            P("dom", "cuts", None, None),
            P("dom", "cuts", None),
            P("dom", "cuts", None),
            P("dom", "cuts", None),
            P("dom", "cuts"),
            P("dom", "cuts", None, None, None),
        ),
        out_specs=P(("dom", "cuts"), None),
        check_vma=False,
    )
```

```python
import jax
import jax.numpy as jnp
from jax import lax
from jax.experimental import pallas as pl
from jax.experimental.pallas import tpu as pltpu
from jax.sharding import PartitionSpec as P

ROWS = 384
SLOT = 16
HUB = 16
BLOCK = 128
CHUNK = 16
CORES = 2
DEAD = 2.0**100
DEAD_LIMIT = 2.0**50
VMEM = pltpu.VMEM
SMEM = pltpu.SMEM
F32 = jnp.float32
BF16 = jnp.bfloat16


def spec(space):
    return pl.BlockSpec(memory_space=space)


LIMIT = 40 * 1024 * 1024


def call(body, out_shape, spaces, scratch=()):
    return pl.pallas_call(
        body,
        out_shape=out_shape,
        in_specs=[spec(s) for s in spaces],
        out_specs=jax.tree.map(lambda _: spec(VMEM), out_shape),
        scratch_shapes=list(scratch),
        compiler_params=pltpu.CompilerParams(vmem_limit_bytes=LIMIT),
    )


def column(row, size):
    here = lax.broadcasted_iota(jnp.int32, (size, size), 0)
    there = lax.broadcasted_iota(jnp.int32, (size, size), 1)
    return jnp.sum(jnp.where(here == there, row, 0), axis=1, keepdims=True)


def one_hot(picks):
    places = lax.broadcasted_iota(jnp.int32, picks.shape, 1)
    return jnp.where(picks == places, 1.0, 0.0).astype(BF16)


def fill_outgoing(table, picks, hub_picks, out, dead):
    parts, slots = picks.shape
    width = table.shape[1]
    hubs = jnp.dot(one_hot(hub_picks), table, preferred_element_type=F32).astype(BF16)
    for first in range(0, parts, CHUNK):
        some = picks[first : first + CHUNK]
        wide = jnp.broadcast_to(some[:, :, None], (CHUNK, slots, ROWS)).reshape(
            CHUNK * slots, ROWS
        )
        rows = jnp.dot(one_hot(wide), table, preferred_element_type=F32)
        if dead != 0.0:
            rows = jnp.where(wide[:, :width] < 0, dead, rows)
        chips = pl.ds(first // CORES, CHUNK // CORES)
        out[chips, : CORES * slots] = rows.astype(BF16).reshape(
            CHUNK // CORES, CORES * slots, width
        )
        out[chips, CORES * slots :] = jnp.broadcast_to(
            hubs[None], (CHUNK // CORES,) + hubs.shape
        )


def pack_body(*refs):
    count = (len(refs) - 4 - 7) // 2
    handed, operands = refs[:count], refs[count : count + 7]
    out, picks_out, hubs_out, plan_out, *handed_out = refs[count + 7 :]
    targets, columns, used, halo_rows, halo_count, hub_rows, table = operands
    slots, parts = halo_rows.shape
    slot = lax.broadcasted_iota(jnp.int32, (slots, parts), 0)
    picks = jnp.where(slot < halo_count[...], halo_rows[...], -1).T
    hub_picks = jnp.broadcast_to(column(hub_rows[...], HUB), (HUB, ROWS))
    picks_out[...] = picks
    hubs_out[...] = hub_picks
    fill_outgoing(table[...], picks, hub_picks, out, 0.0)
    pieces = [targets[...], columns[...], used[...]]
    spare = plan_out.shape[1] - sum(piece.shape[1] for piece in pieces)
    plan_out[...] = jnp.concatenate(
        [*pieces, jnp.zeros((1, spare), jnp.int32)], axis=1
    )
    for source, place in zip(handed, handed_out, strict=True):
        place[...] = source[...]


def pack(handed, *operands):
    slots, parts = operands[-4].shape
    width = operands[-1].shape[1]
    return call(
        pack_body,
        (
            jax.ShapeDtypeStruct((parts // CORES, CORES * SLOT + HUB, width), BF16),
            jax.ShapeDtypeStruct((parts, slots), jnp.int32),
            jax.ShapeDtypeStruct((HUB, ROWS), jnp.int32),
            jax.ShapeDtypeStruct((1, 128), jnp.int32),
            *(jax.ShapeDtypeStruct(x.shape, x.dtype) for x in handed),
        ),
        [VMEM] * (len(handed) + len(operands)),
    )(*handed, *operands)


def sum_body(plan, own, received, passed, tiles, *rest):
    *layer, out, mine, total = rest
    total[...] = jnp.zeros_like(total)
    capacity = tiles.shape[0]
    group = BLOCK // (CORES * SLOT)
    groups = received.shape[0] // group
    core = lax.rem(lax.axis_index("dom"), CORES)
    own_blocks = ROWS // BLOCK
    used = plan[2 * capacity]
    for i in range(capacity):
        col = plan[capacity + i]
        here = jnp.minimum(col, own_blocks - 1)
        local_rows = own[pl.ds(pl.multiple_of(here * BLOCK, BLOCK), BLOCK), :]
        away = jnp.maximum(col - own_blocks, 0)
        hub = jnp.where(away >= groups, 1, 0)
        first = pl.multiple_of((away - hub * groups) * group, group)
        start = pl.multiple_of(jnp.where(hub == 1, CORES * SLOT, core * SLOT), SLOT)
        same = received[pl.ds(first, group), pl.ds(start, SLOT), :]
        other = passed[pl.ds(first, group), pl.ds(start, SLOT), :]
        remote_rows = jnp.stack(
            [jnp.where(core == 0, same, other), jnp.where(core == 0, other, same)],
            axis=1,
        ).reshape(BLOCK, own.shape[1])
        rows = jnp.where(col < own_blocks, local_rows, remote_rows)
        if layer:
            weight, bias = layer
            hidden = jnp.dot(rows, weight[...], preferred_element_type=F32)
            hidden = jnp.maximum(hidden + bias[...], 0.0)
            live = rows.astype(F32) < DEAD_LIMIT
            live = jnp.concatenate([live] * (hidden.shape[1] // live.shape[1]), axis=1)
            rows = jnp.where(live, hidden, 0.0).astype(BF16)
        term = jnp.dot(tiles[i], rows, preferred_element_type=F32)
        row = plan[i]
        total[row] = total[row] + jnp.where(i < used, term, 0.0)
    chunk = ROWS // BLOCK
    cut = lax.axis_index("cuts")
    mine[...] = total[pl.ds(cut * chunk, chunk)].reshape(mine.shape)
    out[...] = total[...].astype(BF16).reshape(out.shape)


def tile_sums(own, received, passed, plan, tiles, cuts, *layer):
    width = layer[0].shape[1] if layer else own.shape[1]
    return call(
        sum_body,
        (
            jax.ShapeDtypeStruct((cuts, ROWS, width), BF16),
            jax.ShapeDtypeStruct((ROWS, width), F32),
        ),
        [SMEM] + [VMEM] * (4 + len(layer)),
        [pltpu.VMEM((cuts * ROWS // BLOCK, BLOCK, width), F32)],
    )(plan, own, received, passed, tiles, *layer)


def over_cuts(parts, mine):
    cut = lax.axis_index("cuts")
    total = mine[...]
    for k in range(parts.shape[0]):
        total = total + jnp.where(cut == k, 0.0, parts[k].astype(F32))
    return total


def middle_body(parts, mine, picks, hub_picks, table, out):
    rows = over_cuts(parts, mine).astype(BF16)
    table[...] = rows
    fill_outgoing(rows, picks[...], hub_picks[...], out, DEAD)


def middle(parts, mine, picks, hub_picks):
    width = mine.shape[1]
    return call(
        middle_body,
        (
            jax.ShapeDtypeStruct((ROWS, width), BF16),
            jax.ShapeDtypeStruct((picks.shape[0] // CORES, CORES * SLOT + HUB, width), BF16),
        ),
        [VMEM] * 4,
    )(parts, mine, picks, hub_picks)


def last_body(parts, mine, weight, bias, out):
    total = over_cuts(parts, mine)
    high = total.astype(BF16)
    low = (total - high.astype(F32)).astype(BF16)
    hidden = jnp.dot(high, weight[...], preferred_element_type=F32) + jnp.dot(
        low, weight[...], preferred_element_type=F32
    )
    out[...] = jnp.maximum(hidden + bias[...], 0.0).astype(BF16)


def swap(rows, axis):
    return lax.all_to_all(rows, axis, split_axis=0, concat_axis=0, tiled=True)


def exchange(rows):
    size = lax.axis_size("dom")
    alike = [list(range(core, size, CORES)) for core in range(CORES)]
    received = lax.all_to_all(
        rows, "dom", split_axis=0, concat_axis=0, tiled=True, axis_index_groups=alike
    )
    return received, lax.ppermute(received, "dom", [(i, i ^ 1) for i in range(size)])


def local(
    features,
    weight_one,
    bias_one,
    weight_two,
    bias_two,
    hub_rows,
    halo_rows,
    halo_count,
    tile_target,
    tile_source,
    tile_count,
    tile_values,
):
    cuts = lax.axis_size("cuts")
    halo_rows = halo_rows.reshape(halo_rows.shape[2:]).T
    tiles = tile_values.reshape(tile_values.shape[2:])
    row = lambda x: x.reshape(1, -1)
    outgoing, picks, hub_picks, plan, bias_one, bias_two = pack(
        (row(bias_one), row(bias_two)),
        row(tile_target),
        row(tile_source),
        row(tile_count),
        halo_rows,
        row(halo_count),
        row(hub_rows),
        features,
    )
    plan = plan.reshape(-1)
    parts, mine = tile_sums(features, *exchange(outgoing), plan, tiles, cuts)
    table, outgoing = middle(swap(parts, "cuts"), mine, picks, hub_picks)
    parts, mine = tile_sums(
        table, *exchange(outgoing), plan, tiles, cuts, weight_one, bias_one
    )
    return call(
        last_body,
        jax.ShapeDtypeStruct((ROWS, weight_two.shape[1]), BF16),
        [VMEM] * 4,
    )(swap(parts, "cuts"), mine, weight_two, bias_two)


def solution(mesh):
    return jax.shard_map(
        local,
        mesh=mesh,
        in_specs=(
            P(("dom", "cuts"), None),
            P(),
            P(),
            P(),
            P(),
            P("dom", "cuts", None),
            P("dom", "cuts", None, None),
            P("dom", "cuts", None),
            P("dom", "cuts", None),
            P("dom", "cuts", None),
            P("dom", "cuts"),
            P("dom", "cuts", None, None, None),
        ),
        out_specs=P(("dom", "cuts"), None),
        check_vma=False,
    )
```

```python
import jax
import jax.numpy as jnp
from jax import lax
from jax.experimental import pallas as pl
from jax.experimental.pallas import tpu as pltpu
from jax.sharding import PartitionSpec as P

ROWS = 384
SLOT = 16
HUB = 16
BLOCK = 128
CHUNK = 16
CORES = 2
DEAD = 2.0**100
DEAD_LIMIT = 2.0**50
VMEM = pltpu.VMEM
SMEM = pltpu.SMEM
F32 = jnp.float32
BF16 = jnp.bfloat16


def spec(space):
    return pl.BlockSpec(memory_space=space)


LIMIT = 40 * 1024 * 1024


def call(body, out_shape, spaces, scratch=(), cost=None):
    return pl.pallas_call(
        body,
        out_shape=out_shape,
        in_specs=[spec(s) for s in spaces],
        out_specs=jax.tree.map(lambda _: spec(VMEM), out_shape),
        scratch_shapes=list(scratch),
        cost_estimate=cost,
        compiler_params=pltpu.CompilerParams(vmem_limit_bytes=LIMIT),
    )


def column(row, size):
    here = lax.broadcasted_iota(jnp.int32, (size, size), 0)
    there = lax.broadcasted_iota(jnp.int32, (size, size), 1)
    return jnp.sum(jnp.where(here == there, row, 0), axis=1, keepdims=True)


def one_hot(picks):
    places = lax.broadcasted_iota(jnp.int32, picks.shape, 1)
    return jnp.where(picks == places, 1.0, 0.0).astype(BF16)


def fill_outgoing(table, picks, hub_picks, out, dead):
    parts, slots = picks.shape
    width = table.shape[1]
    hubs = jnp.dot(one_hot(hub_picks), table, preferred_element_type=F32).astype(BF16)
    for first in range(0, parts, CHUNK):
        some = picks[first : first + CHUNK]
        wide = jnp.broadcast_to(some[:, :, None], (CHUNK, slots, ROWS)).reshape(
            CHUNK * slots, ROWS
        )
        rows = jnp.dot(one_hot(wide), table, preferred_element_type=F32)
        if dead != 0.0:
            rows = jnp.where(wide[:, :width] < 0, dead, rows)
        chips = pl.ds(first // CORES, CHUNK // CORES)
        out[chips, : CORES * slots] = rows.astype(BF16).reshape(
            CHUNK // CORES, CORES * slots, width
        )
        out[chips, CORES * slots :] = jnp.broadcast_to(
            hubs[None], (CHUNK // CORES,) + hubs.shape
        )


def spread_body(number, out):
    out[...] = jnp.full(out.shape, number[0, 0], jnp.int32)


def spread(number):
    return call(
        spread_body,
        jax.ShapeDtypeStruct((1, 128), jnp.int32),
        [SMEM],
        cost=pl.CostEstimate(flops=10**9, bytes_accessed=4 * 10**6, transcendentals=0),
    )(number)


def pack_body(*refs):
    count = (len(refs) - 4 - 7) // 2
    handed, operands = refs[:count], refs[count : count + 7]
    out, picks_out, hubs_out, plan_out, *handed_out = refs[count + 7 :]
    targets, columns, used, halo_rows, halo_count, hub_rows, table = operands
    slots, parts = halo_rows.shape
    slot = lax.broadcasted_iota(jnp.int32, (slots, parts), 0)
    picks = jnp.where(slot < halo_count[...], halo_rows[...], -1).T
    hub_picks = jnp.broadcast_to(column(hub_rows[...], HUB), (HUB, ROWS))
    picks_out[...] = picks
    hubs_out[...] = hub_picks
    fill_outgoing(table[...], picks, hub_picks, out, 0.0)
    capacity = targets.shape[1]
    plan_out[...] = used[...]
    plan_out[:, :capacity] = targets[...]
    plan_out[:, capacity : 2 * capacity] = columns[...]
    for source, place in zip(handed, handed_out, strict=True):
        place[...] = source[...]


def pack(handed, *operands):
    slots, parts = operands[-4].shape
    width = operands[-1].shape[1]
    return call(
        pack_body,
        (
            jax.ShapeDtypeStruct((parts // CORES, CORES * SLOT + HUB, width), BF16),
            jax.ShapeDtypeStruct((parts, slots), jnp.int32),
            jax.ShapeDtypeStruct((HUB, ROWS), jnp.int32),
            jax.ShapeDtypeStruct((1, 128), jnp.int32),
            *(jax.ShapeDtypeStruct(x.shape, x.dtype) for x in handed),
        ),
        [VMEM] * (len(handed) + len(operands)),
    )(*handed, *operands)


def sum_body(plan, own, received, passed, tiles, *rest):
    *layer, out, mine, total = rest
    total[...] = jnp.zeros_like(total)
    capacity = tiles.shape[0]
    group = BLOCK // (CORES * SLOT)
    groups = received.shape[0] // group
    core = lax.rem(lax.axis_index("dom"), CORES)
    own_blocks = ROWS // BLOCK
    used = plan[2 * capacity]
    for i in range(capacity):
        col = plan[capacity + i]
        here = jnp.minimum(col, own_blocks - 1)
        local_rows = own[pl.ds(pl.multiple_of(here * BLOCK, BLOCK), BLOCK), :]
        away = jnp.maximum(col - own_blocks, 0)
        hub = jnp.where(away >= groups, 1, 0)
        first = pl.multiple_of((away - hub * groups) * group, group)
        start = pl.multiple_of(jnp.where(hub == 1, CORES * SLOT, core * SLOT), SLOT)
        same = received[pl.ds(first, group), pl.ds(start, SLOT), :]
        other = passed[pl.ds(first, group), pl.ds(start, SLOT), :]
        remote_rows = jnp.stack(
            [jnp.where(core == 0, same, other), jnp.where(core == 0, other, same)],
            axis=1,
        ).reshape(BLOCK, own.shape[1])
        rows = jnp.where(col < own_blocks, local_rows, remote_rows)
        if layer:
            weight, bias = layer
            hidden = jnp.dot(rows, weight[...], preferred_element_type=F32)
            hidden = jnp.maximum(hidden + bias[...], 0.0)
            live = rows.astype(F32) < DEAD_LIMIT
            live = jnp.concatenate([live] * (hidden.shape[1] // live.shape[1]), axis=1)
            rows = jnp.where(live, hidden, 0.0).astype(BF16)
        term = jnp.dot(tiles[i], rows, preferred_element_type=F32)
        row = plan[i]
        total[row] = total[row] + jnp.where(i < used, term, 0.0)
    chunk = ROWS // BLOCK
    cut = lax.axis_index("cuts")
    mine[...] = total[pl.ds(cut * chunk, chunk)].reshape(mine.shape)
    out[...] = total[...].astype(BF16).reshape(out.shape)


def tile_sums(own, received, passed, plan, tiles, cuts, *layer):
    width = layer[0].shape[1] if layer else own.shape[1]
    return call(
        sum_body,
        (
            jax.ShapeDtypeStruct((cuts, ROWS, width), BF16),
            jax.ShapeDtypeStruct((ROWS, width), F32),
        ),
        [SMEM] + [VMEM] * (4 + len(layer)),
        [pltpu.VMEM((cuts * ROWS // BLOCK, BLOCK, width), F32)],
    )(plan, own, received, passed, tiles, *layer)


def over_cuts(parts, mine):
    cut = lax.axis_index("cuts")
    total = mine[...]
    for k in range(parts.shape[0]):
        total = total + jnp.where(cut == k, 0.0, parts[k].astype(F32))
    return total


def middle_body(parts, mine, picks, hub_picks, table, out):
    rows = over_cuts(parts, mine).astype(BF16)
    table[...] = rows
    fill_outgoing(rows, picks[...], hub_picks[...], out, DEAD)


def middle(parts, mine, picks, hub_picks):
    width = mine.shape[1]
    return call(
        middle_body,
        (
            jax.ShapeDtypeStruct((ROWS, width), BF16),
            jax.ShapeDtypeStruct((picks.shape[0] // CORES, CORES * SLOT + HUB, width), BF16),
        ),
        [VMEM] * 4,
    )(parts, mine, picks, hub_picks)


def last_body(parts, mine, weight, bias, out):
    total = over_cuts(parts, mine)
    high = total.astype(BF16)
    low = (total - high.astype(F32)).astype(BF16)
    hidden = jnp.dot(high, weight[...], preferred_element_type=F32) + jnp.dot(
        low, weight[...], preferred_element_type=F32
    )
    out[...] = jnp.maximum(hidden + bias[...], 0.0).astype(BF16)


def swap(rows, axis):
    return lax.all_to_all(rows, axis, split_axis=0, concat_axis=0, tiled=True)


def exchange(rows):
    size = lax.axis_size("dom")
    alike = [list(range(core, size, CORES)) for core in range(CORES)]
    received = lax.all_to_all(
        rows, "dom", split_axis=0, concat_axis=0, tiled=True, axis_index_groups=alike
    )
    return received, lax.ppermute(received, "dom", [(i, i ^ 1) for i in range(size)])


def local(
    features,
    weight_one,
    bias_one,
    weight_two,
    bias_two,
    hub_rows,
    halo_rows,
    halo_count,
    tile_target,
    tile_source,
    tile_count,
    tile_values,
):
    cuts = lax.axis_size("cuts")
    halo_rows = halo_rows.reshape(halo_rows.shape[2:]).T
    tiles = tile_values.reshape(tile_values.shape[2:])
    row = lambda x: x.reshape(1, -1)
    outgoing, picks, hub_picks, plan, bias_one, bias_two = pack(
        (row(bias_one), row(bias_two)),
        row(tile_target),
        row(tile_source),
        spread(row(tile_count)),
        halo_rows,
        row(halo_count),
        row(hub_rows),
        features,
    )
    plan = plan.reshape(-1)
    parts, mine = tile_sums(features, *exchange(outgoing), plan, tiles, cuts)
    table, outgoing = middle(swap(parts, "cuts"), mine, picks, hub_picks)
    parts, mine = tile_sums(
        table, *exchange(outgoing), plan, tiles, cuts, weight_one, bias_one
    )
    return call(
        last_body,
        jax.ShapeDtypeStruct((ROWS, weight_two.shape[1]), BF16),
        [VMEM] * 4,
    )(swap(parts, "cuts"), mine, weight_two, bias_two)


def solution(mesh):
    return jax.shard_map(
        local,
        mesh=mesh,
        in_specs=(
            P(("dom", "cuts"), None),
            P(),
            P(),
            P(),
            P(),
            P("dom", "cuts", None),
            P("dom", "cuts", None, None),
            P("dom", "cuts", None),
            P("dom", "cuts", None),
            P("dom", "cuts", None),
            P("dom", "cuts"),
            P("dom", "cuts", None, None, None),
        ),
        out_specs=P(("dom", "cuts"), None),
        check_vma=False,
    )
```

```python
import jax
import jax.numpy as jnp
from jax import lax
from jax.experimental import pallas as pl
from jax.experimental.pallas import tpu as pltpu
from jax.sharding import PartitionSpec as P

ROWS = 384
SLOT = 16
HUB = 16
BLOCK = 128
CHUNK = 16
CORES = 2
DEAD = 2.0**100
DEAD_LIMIT = 2.0**50
VMEM = pltpu.VMEM
SMEM = pltpu.SMEM
F32 = jnp.float32
BF16 = jnp.bfloat16


def spec(space):
    return pl.BlockSpec(memory_space=space)


LIMIT = 40 * 1024 * 1024


def call(body, out_shape, spaces, scratch=(), cost=None):
    return pl.pallas_call(
        body,
        out_shape=out_shape,
        in_specs=[spec(s) for s in spaces],
        out_specs=jax.tree.map(lambda _: spec(VMEM), out_shape),
        scratch_shapes=list(scratch),
        cost_estimate=cost,
        compiler_params=pltpu.CompilerParams(vmem_limit_bytes=LIMIT),
    )


def column(row, size):
    here = lax.broadcasted_iota(jnp.int32, (size, size), 0)
    there = lax.broadcasted_iota(jnp.int32, (size, size), 1)
    return jnp.sum(jnp.where(here == there, row, 0), axis=1, keepdims=True)


def one_hot(picks):
    places = lax.broadcasted_iota(jnp.int32, picks.shape, 1)
    return jnp.where(picks == places, 1.0, 0.0).astype(BF16)


def fill_outgoing(table, picks, hub_picks, out, dead):
    parts, slots = picks.shape
    width = table.shape[1]
    hubs = jnp.dot(one_hot(hub_picks), table, preferred_element_type=F32).astype(BF16)
    for first in range(0, parts, CHUNK):
        some = picks[first : first + CHUNK]
        wide = jnp.broadcast_to(some[:, :, None], (CHUNK, slots, ROWS)).reshape(
            CHUNK * slots, ROWS
        )
        rows = jnp.dot(one_hot(wide), table, preferred_element_type=F32)
        if dead != 0.0:
            rows = jnp.where(wide[:, :width] < 0, dead, rows)
        chips = pl.ds(first // CORES, CHUNK // CORES)
        out[chips, : CORES * slots] = rows.astype(BF16).reshape(
            CHUNK // CORES, CORES * slots, width
        )
        out[chips, CORES * slots :] = jnp.broadcast_to(
            hubs[None], (CHUNK // CORES,) + hubs.shape
        )


def slots_body(out):
    out[...] = lax.broadcasted_iota(jnp.int32, out.shape, 0)


def slot_numbers(slots, parts):
    return call(
        slots_body,
        jax.ShapeDtypeStruct((slots, parts), jnp.int32),
        [],
        cost=pl.CostEstimate(flops=10**9, bytes_accessed=4 * 10**6, transcendentals=0),
    )()


def pack_body(*refs):
    count = (len(refs) - 3 - 5) // 2
    handed, (slot, halo_rows, halo_count, hub_rows, table) = refs[:count], refs[count : count + 5]
    out, picks_out, hubs_out, *handed_out = refs[count + 5 :]
    picks = jnp.where(slot[...] < halo_count[...], halo_rows[...], -1).T
    hub_picks = jnp.broadcast_to(column(hub_rows[...], HUB), (HUB, ROWS))
    picks_out[...] = picks
    hubs_out[...] = hub_picks
    fill_outgoing(table[...], picks, hub_picks, out, 0.0)
    for source, place in zip(handed, handed_out, strict=True):
        place[...] = source[...]


def pack(handed, halo_rows, halo_count, hub_rows, table):
    slots, parts = halo_rows.shape
    operands = (slot_numbers(slots, parts), halo_rows, halo_count, hub_rows, table)
    return call(
        pack_body,
        (
            jax.ShapeDtypeStruct(
                (parts // CORES, CORES * SLOT + HUB, table.shape[1]), BF16
            ),
            jax.ShapeDtypeStruct((parts, slots), jnp.int32),
            jax.ShapeDtypeStruct((HUB, ROWS), jnp.int32),
            *(jax.ShapeDtypeStruct(x.shape, x.dtype) for x in handed),
        ),
        [VMEM] * (len(handed) + len(operands)),
    )(*handed, *operands)


def plan_body(targets, columns, used, out):
    capacity = targets.shape[1]
    out[...] = jnp.broadcast_to(used[...], out.shape)
    out[:, :capacity] = targets[...]
    out[:, capacity : 2 * capacity] = columns[...]


def tile_plan(targets, columns, used):
    return call(
        plan_body, jax.ShapeDtypeStruct((1, 128), jnp.int32), [VMEM] * 3
    )(targets, columns, used)


def sum_body(plan, own, received, passed, tiles, *rest):
    *layer, out, mine, total = rest
    total[...] = jnp.zeros_like(total)
    capacity = tiles.shape[0]
    group = BLOCK // (CORES * SLOT)
    groups = received.shape[0] // group
    core = lax.rem(lax.axis_index("dom"), CORES)
    own_blocks = ROWS // BLOCK
    used = plan[2 * capacity]
    for i in range(capacity):
        col = plan[capacity + i]
        here = jnp.minimum(col, own_blocks - 1)
        local_rows = own[pl.ds(pl.multiple_of(here * BLOCK, BLOCK), BLOCK), :]
        away = jnp.maximum(col - own_blocks, 0)
        hub = jnp.where(away >= groups, 1, 0)
        first = pl.multiple_of((away - hub * groups) * group, group)
        start = pl.multiple_of(jnp.where(hub == 1, CORES * SLOT, core * SLOT), SLOT)
        same = received[pl.ds(first, group), pl.ds(start, SLOT), :]
        other = passed[pl.ds(first, group), pl.ds(start, SLOT), :]
        remote_rows = jnp.stack(
            [jnp.where(core == 0, same, other), jnp.where(core == 0, other, same)],
            axis=1,
        ).reshape(BLOCK, own.shape[1])
        rows = jnp.where(col < own_blocks, local_rows, remote_rows)
        if layer:
            weight, bias = layer
            hidden = jnp.dot(rows, weight[...], preferred_element_type=F32)
            hidden = jnp.maximum(hidden + bias[...], 0.0)
            live = rows.astype(F32) < DEAD_LIMIT
            live = jnp.concatenate([live] * (hidden.shape[1] // live.shape[1]), axis=1)
            rows = jnp.where(live, hidden, 0.0).astype(BF16)
        term = jnp.dot(tiles[i], rows, preferred_element_type=F32)
        row = plan[i]
        total[row] = total[row] + jnp.where(i < used, term, 0.0)
    chunk = ROWS // BLOCK
    cut = lax.axis_index("cuts")
    mine[...] = total[pl.ds(cut * chunk, chunk)].reshape(mine.shape)
    out[...] = total[...].astype(BF16).reshape(out.shape)


def tile_sums(own, received, passed, plan, tiles, cuts, *layer):
    width = layer[0].shape[1] if layer else own.shape[1]
    return call(
        sum_body,
        (
            jax.ShapeDtypeStruct((cuts, ROWS, width), BF16),
            jax.ShapeDtypeStruct((ROWS, width), F32),
        ),
        [SMEM] + [VMEM] * (4 + len(layer)),
        [pltpu.VMEM((cuts * ROWS // BLOCK, BLOCK, width), F32)],
    )(plan, own, received, passed, tiles, *layer)


def over_cuts(parts, mine):
    cut = lax.axis_index("cuts")
    total = mine[...]
    for k in range(parts.shape[0]):
        total = total + jnp.where(cut == k, 0.0, parts[k].astype(F32))
    return total


def middle_body(parts, mine, picks, hub_picks, table, out):
    rows = over_cuts(parts, mine).astype(BF16)
    table[...] = rows
    fill_outgoing(rows, picks[...], hub_picks[...], out, DEAD)


def middle(parts, mine, picks, hub_picks):
    width = mine.shape[1]
    return call(
        middle_body,
        (
            jax.ShapeDtypeStruct((ROWS, width), BF16),
            jax.ShapeDtypeStruct((picks.shape[0] // CORES, CORES * SLOT + HUB, width), BF16),
        ),
        [VMEM] * 4,
    )(parts, mine, picks, hub_picks)


def last_body(parts, mine, weight, bias, out):
    total = over_cuts(parts, mine)
    high = total.astype(BF16)
    low = (total - high.astype(F32)).astype(BF16)
    hidden = jnp.dot(high, weight[...], preferred_element_type=F32) + jnp.dot(
        low, weight[...], preferred_element_type=F32
    )
    out[...] = jnp.maximum(hidden + bias[...], 0.0).astype(BF16)


def swap(rows, axis):
    return lax.all_to_all(rows, axis, split_axis=0, concat_axis=0, tiled=True)


def exchange(rows):
    size = lax.axis_size("dom")
    alike = [list(range(core, size, CORES)) for core in range(CORES)]
    received = lax.all_to_all(
        rows, "dom", split_axis=0, concat_axis=0, tiled=True, axis_index_groups=alike
    )
    return received, lax.ppermute(received, "dom", [(i, i ^ 1) for i in range(size)])


def local(
    features,
    weight_one,
    bias_one,
    weight_two,
    bias_two,
    hub_rows,
    halo_rows,
    halo_count,
    tile_target,
    tile_source,
    tile_count,
    tile_values,
):
    cuts = lax.axis_size("cuts")
    halo_rows = halo_rows.reshape(halo_rows.shape[2:]).T
    tiles = tile_values.reshape(tile_values.shape[2:])
    row = lambda x: x.reshape(1, -1)
    outgoing, picks, hub_picks, bias_one, bias_two = pack(
        (row(bias_one), row(bias_two)),
        halo_rows,
        row(halo_count),
        row(hub_rows),
        features,
    )
    plan = tile_plan(row(tile_target), row(tile_source), row(tile_count)).reshape(-1)
    parts, mine = tile_sums(features, *exchange(outgoing), plan, tiles, cuts)
    table, outgoing = middle(swap(parts, "cuts"), mine, picks, hub_picks)
    parts, mine = tile_sums(
        table, *exchange(outgoing), plan, tiles, cuts, weight_one, bias_one
    )
    return call(
        last_body,
        jax.ShapeDtypeStruct((ROWS, weight_two.shape[1]), BF16),
        [VMEM] * 4,
    )(swap(parts, "cuts"), mine, weight_two, bias_two)


def solution(mesh):
    return jax.shard_map(
        local,
        mesh=mesh,
        in_specs=(
            P(("dom", "cuts"), None),
            P(),
            P(),
            P(),
            P(),
            P("dom", "cuts", None),
            P("dom", "cuts", None, None),
            P("dom", "cuts", None),
            P("dom", "cuts", None),
            P("dom", "cuts", None),
            P("dom", "cuts"),
            P("dom", "cuts", None, None, None),
        ),
        out_specs=P(("dom", "cuts"), None),
        check_vma=False,
    )
```

```python
import functools

import jax
import jax.numpy as jnp
from jax import lax
from jax.experimental import pallas as pl
from jax.experimental.pallas import tpu as pltpu
from jax.sharding import PartitionSpec as P

ROWS = 384
SLOT = 16
HUB = 16
BLOCK = 128
CHUNK = 16
CORES = 2
HIDDEN_ROWS = 512
DEAD = 2.0**100
DEAD_LIMIT = 2.0**50
VMEM = pltpu.VMEM
SMEM = pltpu.SMEM
F32 = jnp.float32
BF16 = jnp.bfloat16


def spec(space):
    return pl.BlockSpec(memory_space=space)


LIMIT = 40 * 1024 * 1024


def call(body, out_shape, spaces, scratch=(), cost=None):
    return pl.pallas_call(
        body,
        out_shape=out_shape,
        in_specs=[spec(s) for s in spaces],
        out_specs=jax.tree.map(lambda _: spec(VMEM), out_shape),
        scratch_shapes=list(scratch),
        cost_estimate=cost,
        compiler_params=pltpu.CompilerParams(vmem_limit_bytes=LIMIT),
    )


def column(row, size):
    here = lax.broadcasted_iota(jnp.int32, (size, size), 0)
    there = lax.broadcasted_iota(jnp.int32, (size, size), 1)
    return jnp.sum(jnp.where(here == there, row, 0), axis=1, keepdims=True)


def one_hot(picks):
    places = lax.broadcasted_iota(jnp.int32, picks.shape, 1)
    return jnp.where(picks == places, 1.0, 0.0).astype(BF16)


def fill_outgoing(table, picks, hub_picks, out, dead):
    parts, slots = picks.shape
    width = table.shape[1]
    hubs = jnp.dot(one_hot(hub_picks), table, preferred_element_type=F32).astype(BF16)
    for first in range(0, parts, CHUNK):
        some = picks[first : first + CHUNK]
        wide = jnp.broadcast_to(some[:, :, None], (CHUNK, slots, ROWS)).reshape(
            CHUNK * slots, ROWS
        )
        rows = jnp.dot(one_hot(wide), table, preferred_element_type=F32)
        if dead != 0.0:
            rows = jnp.where(wide[:, :width] < 0, dead, rows)
        chips = pl.ds(first // CORES, CHUNK // CORES)
        out[chips, : CORES * slots] = rows.astype(BF16).reshape(
            CHUNK // CORES, CORES * slots, width
        )
        out[chips, CORES * slots :] = jnp.broadcast_to(
            hubs[None], (CHUNK // CORES,) + hubs.shape
        )


def slots_body(out):
    out[...] = lax.broadcasted_iota(jnp.int32, out.shape, 0)


def slot_numbers(slots, parts):
    return call(
        slots_body,
        jax.ShapeDtypeStruct((slots, parts), jnp.int32),
        [],
        cost=pl.CostEstimate(flops=10**9, bytes_accessed=4 * 10**6, transcendentals=0),
    )()


def pack_body(*refs):
    count = (len(refs) - 3 - 5) // 2
    handed, (slot, halo_rows, halo_count, hub_rows, table) = refs[:count], refs[count : count + 5]
    out, picks_out, hubs_out, *handed_out = refs[count + 5 :]
    picks = jnp.where(slot[...] < halo_count[...], halo_rows[...], -1).T
    hub_picks = jnp.broadcast_to(column(hub_rows[...], HUB), (HUB, ROWS))
    picks_out[...] = picks
    hubs_out[...] = hub_picks
    fill_outgoing(table[...], picks, hub_picks, out, 0.0)
    for source, place in zip(handed, handed_out, strict=True):
        place[...] = source[...]


def pack(handed, halo_rows, halo_count, hub_rows, table):
    slots, parts = halo_rows.shape
    operands = (slot_numbers(slots, parts), halo_rows, halo_count, hub_rows, table)
    return call(
        pack_body,
        (
            jax.ShapeDtypeStruct(
                (parts // CORES, CORES * SLOT + HUB, table.shape[1]), BF16
            ),
            jax.ShapeDtypeStruct((parts, slots), jnp.int32),
            jax.ShapeDtypeStruct((HUB, ROWS), jnp.int32),
            *(jax.ShapeDtypeStruct(x.shape, x.dtype) for x in handed),
        ),
        [VMEM] * (len(handed) + len(operands)),
    )(*handed, *operands)


def plan_body(targets, columns, used, out):
    capacity = targets.shape[1]
    out[...] = jnp.broadcast_to(used[...], out.shape)
    out[:, :capacity] = targets[...]
    out[:, capacity : 2 * capacity] = columns[...]


def tile_plan(targets, columns, used):
    return call(
        plan_body, jax.ShapeDtypeStruct((1, 128), jnp.int32), [VMEM] * 3
    )(targets, columns, used)


def sum_body(layers, plan, own, received, passed, tiles, *rest):
    layer, (out, mine, total, *scratch) = rest[:layers], rest[layers:]
    total[...] = jnp.zeros_like(total)
    capacity = tiles.shape[0]
    group = BLOCK // (CORES * SLOT)
    groups = received.shape[0] // group
    core = lax.rem(lax.axis_index("dom"), CORES)
    own_blocks = ROWS // BLOCK
    used = plan[2 * capacity]

    def source_rows(i):
        col = plan[capacity + i]
        here = jnp.minimum(col, own_blocks - 1)
        local_rows = own[pl.ds(pl.multiple_of(here * BLOCK, BLOCK), BLOCK), :]
        away = jnp.maximum(col - own_blocks, 0)
        hub = jnp.where(away >= groups, 1, 0)
        first = pl.multiple_of((away - hub * groups) * group, group)
        start = pl.multiple_of(jnp.where(hub == 1, CORES * SLOT, core * SLOT), SLOT)
        same = received[pl.ds(first, group), pl.ds(start, SLOT), :]
        other = passed[pl.ds(first, group), pl.ds(start, SLOT), :]
        remote_rows = jnp.stack(
            [jnp.where(core == 0, same, other), jnp.where(core == 0, other, same)],
            axis=1,
        ).reshape(BLOCK, own.shape[1])
        return jnp.where(col < own_blocks, local_rows, remote_rows)

    if layer:
        (weight, bias), (picked, values) = layer, scratch
        for i in range(capacity):
            picked[i * BLOCK : (i + 1) * BLOCK] = source_rows(i)
        for first in range(0, capacity * BLOCK, HIDDEN_ROWS):
            span = pl.ds(first, HIDDEN_ROWS)
            rows = picked[span]
            hidden = jnp.dot(rows, weight[...], preferred_element_type=F32)
            hidden = jnp.maximum(hidden + bias[...], 0.0)
            live = rows.astype(F32) < DEAD_LIMIT
            live = jnp.concatenate([live] * (hidden.shape[1] // live.shape[1]), axis=1)
            values[span] = jnp.where(live, hidden, 0.0).astype(BF16)
    for i in range(capacity):
        rows = values[i * BLOCK : (i + 1) * BLOCK] if layer else source_rows(i)
        term = jnp.dot(tiles[i], rows, preferred_element_type=F32)
        row = plan[i]
        total[row] = total[row] + jnp.where(i < used, term, 0.0)
    chunk = ROWS // BLOCK
    cut = lax.axis_index("cuts")
    mine[...] = total[pl.ds(cut * chunk, chunk)].reshape(mine.shape)
    out[...] = total[...].astype(BF16).reshape(out.shape)


def tile_sums(own, received, passed, plan, tiles, cuts, *layer):
    width = layer[0].shape[1] if layer else own.shape[1]
    rows = tiles.shape[0] * BLOCK
    scratch = [pltpu.VMEM((cuts * ROWS // BLOCK, BLOCK, width), F32)]
    if layer:
        scratch += [pltpu.VMEM((rows, own.shape[1]), BF16), pltpu.VMEM((rows, width), BF16)]
    return call(
        functools.partial(sum_body, len(layer)),
        (
            jax.ShapeDtypeStruct((cuts, ROWS, width), BF16),
            jax.ShapeDtypeStruct((ROWS, width), F32),
        ),
        [SMEM] + [VMEM] * (4 + len(layer)),
        scratch,
    )(plan, own, received, passed, tiles, *layer)


def over_cuts(parts, mine):
    cut = lax.axis_index("cuts")
    total = mine[...]
    for k in range(parts.shape[0]):
        total = total + jnp.where(cut == k, 0.0, parts[k].astype(F32))
    return total


def middle_body(parts, mine, picks, hub_picks, table, out):
    rows = over_cuts(parts, mine).astype(BF16)
    table[...] = rows
    fill_outgoing(rows, picks[...], hub_picks[...], out, DEAD)


def middle(parts, mine, picks, hub_picks):
    width = mine.shape[1]
    return call(
        middle_body,
        (
            jax.ShapeDtypeStruct((ROWS, width), BF16),
            jax.ShapeDtypeStruct((picks.shape[0] // CORES, CORES * SLOT + HUB, width), BF16),
        ),
        [VMEM] * 4,
    )(parts, mine, picks, hub_picks)


def last_body(parts, mine, weight, bias, out):
    total = over_cuts(parts, mine)
    high = total.astype(BF16)
    low = (total - high.astype(F32)).astype(BF16)
    hidden = jnp.dot(high, weight[...], preferred_element_type=F32) + jnp.dot(
        low, weight[...], preferred_element_type=F32
    )
    out[...] = jnp.maximum(hidden + bias[...], 0.0).astype(BF16)


def swap(rows, axis):
    return lax.all_to_all(rows, axis, split_axis=0, concat_axis=0, tiled=True)


def exchange(rows):
    size = lax.axis_size("dom")
    alike = [list(range(core, size, CORES)) for core in range(CORES)]
    received = lax.all_to_all(
        rows, "dom", split_axis=0, concat_axis=0, tiled=True, axis_index_groups=alike
    )
    return received, lax.ppermute(received, "dom", [(i, i ^ 1) for i in range(size)])


def local(
    features,
    weight_one,
    bias_one,
    weight_two,
    bias_two,
    hub_rows,
    halo_rows,
    halo_count,
    tile_target,
    tile_source,
    tile_count,
    tile_values,
):
    cuts = lax.axis_size("cuts")
    halo_rows = halo_rows.reshape(halo_rows.shape[2:]).T
    tiles = tile_values.reshape(tile_values.shape[2:])
    row = lambda x: x.reshape(1, -1)
    outgoing, picks, hub_picks, bias_one, bias_two = pack(
        (row(bias_one), row(bias_two)),
        halo_rows,
        row(halo_count),
        row(hub_rows),
        features,
    )
    plan = tile_plan(row(tile_target), row(tile_source), row(tile_count)).reshape(-1)
    parts, mine = tile_sums(features, *exchange(outgoing), plan, tiles, cuts)
    table, outgoing = middle(swap(parts, "cuts"), mine, picks, hub_picks)
    parts, mine = tile_sums(
        table, *exchange(outgoing), plan, tiles, cuts, weight_one, bias_one
    )
    return call(
        last_body,
        jax.ShapeDtypeStruct((ROWS, weight_two.shape[1]), BF16),
        [VMEM] * 4,
    )(swap(parts, "cuts"), mine, weight_two, bias_two)


def solution(mesh):
    return jax.shard_map(
        local,
        mesh=mesh,
        in_specs=(
            P(("dom", "cuts"), None),
            P(),
            P(),
            P(),
            P(),
            P("dom", "cuts", None),
            P("dom", "cuts", None, None),
            P("dom", "cuts", None),
            P("dom", "cuts", None),
            P("dom", "cuts", None),
            P("dom", "cuts"),
            P("dom", "cuts", None, None, None),
        ),
        out_specs=P(("dom", "cuts"), None),
        check_vma=False,
    )
```

```python
import jax
import jax.numpy as jnp
from jax import lax
from jax.experimental import pallas as pl
from jax.experimental.pallas import tpu as pltpu
from jax.sharding import PartitionSpec as P

ROWS = 384
SLOT = 16
HUB = 16
BLOCK = 128
CHUNK = 16
CORES = 2
DEAD = 2.0**100
DEAD_LIMIT = 2.0**50
VMEM = pltpu.VMEM
SMEM = pltpu.SMEM
F32 = jnp.float32
BF16 = jnp.bfloat16


def spec(space):
    return pl.BlockSpec(memory_space=space)


LIMIT = 40 * 1024 * 1024


def call(body, out_shape, spaces, scratch=(), cost=None):
    return pl.pallas_call(
        body,
        out_shape=out_shape,
        in_specs=[spec(s) for s in spaces],
        out_specs=jax.tree.map(lambda _: spec(VMEM), out_shape),
        scratch_shapes=list(scratch),
        cost_estimate=cost,
        compiler_params=pltpu.CompilerParams(vmem_limit_bytes=LIMIT),
    )


def column(row, size):
    here = lax.broadcasted_iota(jnp.int32, (size, size), 0)
    there = lax.broadcasted_iota(jnp.int32, (size, size), 1)
    return jnp.sum(jnp.where(here == there, row, 0), axis=1, keepdims=True)


def one_hot(picks):
    places = lax.broadcasted_iota(jnp.int32, picks.shape, 1)
    return jnp.where(picks == places, 1.0, 0.0).astype(BF16)


def fill_outgoing(table, picks, hub_picks, out, dead):
    parts, slots = picks.shape
    width = table.shape[1]
    hubs = jnp.dot(one_hot(hub_picks), table, preferred_element_type=F32).astype(BF16)
    for first in range(0, parts, CHUNK):
        some = picks[first : first + CHUNK]
        wide = jnp.broadcast_to(some[:, :, None], (CHUNK, slots, ROWS)).reshape(
            CHUNK * slots, ROWS
        )
        rows = jnp.dot(one_hot(wide), table, preferred_element_type=F32)
        if dead != 0.0:
            rows = jnp.where(wide[:, :width] < 0, dead, rows)
        chips = pl.ds(first // CORES, CHUNK // CORES)
        out[chips, : CORES * slots] = rows.astype(BF16).reshape(
            CHUNK // CORES, CORES * slots, width
        )
        out[chips, CORES * slots :] = jnp.broadcast_to(
            hubs[None], (CHUNK // CORES,) + hubs.shape
        )


def slots_body(out):
    out[...] = lax.broadcasted_iota(jnp.int32, out.shape, 0)


def slot_numbers(slots, parts):
    return call(
        slots_body,
        jax.ShapeDtypeStruct((slots, parts), jnp.int32),
        [],
        cost=pl.CostEstimate(flops=10**9, bytes_accessed=4 * 10**6, transcendentals=0),
    )()


def pack_body(*refs):
    count = (len(refs) - 3 - 5) // 2
    handed, (slot, halo_rows, halo_count, hub_rows, table) = refs[:count], refs[count : count + 5]
    out, picks_out, hubs_out, *handed_out = refs[count + 5 :]
    picks = jnp.where(slot[...] < halo_count[...], halo_rows[...], -1).T
    hub_picks = jnp.broadcast_to(column(hub_rows[...], HUB), (HUB, ROWS))
    picks_out[...] = picks
    hubs_out[...] = hub_picks
    fill_outgoing(table[...], picks, hub_picks, out, 0.0)
    for source, place in zip(handed, handed_out, strict=True):
        place[...] = source[...]


def pack(handed, halo_rows, halo_count, hub_rows, table):
    slots, parts = halo_rows.shape
    operands = (slot_numbers(slots, parts), halo_rows, halo_count, hub_rows, table)
    return call(
        pack_body,
        (
            jax.ShapeDtypeStruct(
                (parts // CORES, CORES * SLOT + HUB, table.shape[1]), BF16
            ),
            jax.ShapeDtypeStruct((parts, slots), jnp.int32),
            jax.ShapeDtypeStruct((HUB, ROWS), jnp.int32),
            *(jax.ShapeDtypeStruct(x.shape, x.dtype) for x in handed),
        ),
        [VMEM] * (len(handed) + len(operands)),
    )(*handed, *operands)


def plan_body(targets, columns, used, out):
    capacity = targets.shape[1]
    out[...] = jnp.broadcast_to(used[...], out.shape)
    out[:, :capacity] = targets[...]
    out[:, capacity : 2 * capacity] = columns[...]


def tile_plan(targets, columns, used):
    return call(
        plan_body, jax.ShapeDtypeStruct((1, 128), jnp.int32), [VMEM] * 3
    )(targets, columns, used)


def sum_body(plan, own, received, passed, tiles, *rest):
    *layer, out, mine, total = rest
    total[...] = jnp.zeros_like(total)
    capacity = tiles.shape[0]
    group = BLOCK // (CORES * SLOT)
    groups = received.shape[0] // group
    core = lax.axis_index("core")
    own_blocks = ROWS // BLOCK
    used = plan[2 * capacity]
    for i in range(capacity):
        col = plan[capacity + i]
        here = jnp.minimum(col, own_blocks - 1)
        local_rows = own[pl.ds(pl.multiple_of(here * BLOCK, BLOCK), BLOCK), :]
        away = jnp.maximum(col - own_blocks, 0)
        hub = jnp.where(away >= groups, 1, 0)
        first = pl.multiple_of((away - hub * groups) * group, group)
        start = pl.multiple_of(jnp.where(hub == 1, CORES * SLOT, core * SLOT), SLOT)
        same = received[pl.ds(first, group), pl.ds(start, SLOT), :]
        other = passed[pl.ds(first, group), pl.ds(start, SLOT), :]
        remote_rows = jnp.stack(
            [jnp.where(core == 0, same, other), jnp.where(core == 0, other, same)],
            axis=1,
        ).reshape(BLOCK, own.shape[1])
        rows = jnp.where(col < own_blocks, local_rows, remote_rows)
        if layer:
            weight, bias = layer
            hidden = jnp.dot(rows, weight[...], preferred_element_type=F32)
            hidden = jnp.maximum(hidden + bias[...], 0.0)
            live = rows.astype(F32) < DEAD_LIMIT
            live = jnp.concatenate([live] * (hidden.shape[1] // live.shape[1]), axis=1)
            rows = jnp.where(live, hidden, 0.0).astype(BF16)
        term = jnp.dot(tiles[i], rows, preferred_element_type=F32)
        row = plan[i]
        total[row] = total[row] + jnp.where(i < used, term, 0.0)
    chunk = ROWS // BLOCK
    cut = lax.axis_index("cuts")
    mine[...] = total[pl.ds(cut * chunk, chunk)].reshape(mine.shape)
    out[...] = total[...].astype(BF16).reshape(out.shape)


def tile_sums(own, received, passed, plan, tiles, cuts, *layer):
    width = layer[0].shape[1] if layer else own.shape[1]
    return call(
        sum_body,
        (
            jax.ShapeDtypeStruct((cuts, ROWS, width), BF16),
            jax.ShapeDtypeStruct((ROWS, width), F32),
        ),
        [SMEM] + [VMEM] * (4 + len(layer)),
        [pltpu.VMEM((cuts * ROWS // BLOCK, BLOCK, width), F32)],
    )(plan, own, received, passed, tiles, *layer)


def over_cuts(parts, mine):
    cut = lax.axis_index("cuts")
    total = mine[...]
    for k in range(parts.shape[0]):
        total = total + jnp.where(cut == k, 0.0, parts[k].astype(F32))
    return total


def middle_body(parts, mine, picks, hub_picks, table, out):
    rows = over_cuts(parts, mine).astype(BF16)
    table[...] = rows
    fill_outgoing(rows, picks[...], hub_picks[...], out, DEAD)


def middle(parts, mine, picks, hub_picks):
    width = mine.shape[1]
    return call(
        middle_body,
        (
            jax.ShapeDtypeStruct((ROWS, width), BF16),
            jax.ShapeDtypeStruct((picks.shape[0] // CORES, CORES * SLOT + HUB, width), BF16),
        ),
        [VMEM] * 4,
    )(parts, mine, picks, hub_picks)


def last_body(parts, mine, weight, bias, out):
    total = over_cuts(parts, mine)
    high = total.astype(BF16)
    low = (total - high.astype(F32)).astype(BF16)
    hidden = jnp.dot(high, weight[...], preferred_element_type=F32) + jnp.dot(
        low, weight[...], preferred_element_type=F32
    )
    out[...] = jnp.maximum(hidden + bias[...], 0.0).astype(BF16)


def swap(rows, axis):
    return lax.all_to_all(rows, axis, split_axis=0, concat_axis=0, tiled=True)


def exchange(rows):
    received = swap(rows, "chip")
    return received, lax.ppermute(received, "core", [(0, 1), (1, 0)])


def local(
    features,
    weight_one,
    bias_one,
    weight_two,
    bias_two,
    hub_rows,
    halo_rows,
    halo_count,
    tile_target,
    tile_source,
    tile_count,
    tile_values,
):
    cuts = lax.axis_size("cuts")
    halo_rows = halo_rows.reshape(halo_rows.shape[2:]).T
    tiles = tile_values.reshape(tile_values.shape[2:])
    row = lambda x: x.reshape(1, -1)
    outgoing, picks, hub_picks, bias_one, bias_two = pack(
        (row(bias_one), row(bias_two)),
        halo_rows,
        row(halo_count),
        row(hub_rows),
        features,
    )
    plan = tile_plan(row(tile_target), row(tile_source), row(tile_count)).reshape(-1)
    parts, mine = tile_sums(features, *exchange(outgoing), plan, tiles, cuts)
    table, outgoing = middle(swap(parts, "cuts"), mine, picks, hub_picks)
    parts, mine = tile_sums(
        table, *exchange(outgoing), plan, tiles, cuts, weight_one, bias_one
    )
    return call(
        last_body,
        jax.ShapeDtypeStruct((ROWS, weight_two.shape[1]), BF16),
        [VMEM] * 4,
    )(swap(parts, "cuts"), mine, weight_two, bias_two)


def solution(mesh):
    cuts = mesh.shape["cuts"]
    chips = jax.sharding.Mesh(
        mesh.devices.reshape(-1, CORES, cuts), ("chip", "core", "cuts")
    )
    dom = ("chip", "core")
    return jax.shard_map(
        local,
        mesh=chips,
        in_specs=(
            P((*dom, "cuts"), None),
            P(),
            P(),
            P(),
            P(),
            P(dom, "cuts", None),
            P(dom, "cuts", None, None),
            P(dom, "cuts", None),
            P(dom, "cuts", None),
            P(dom, "cuts", None),
            P(dom, "cuts"),
            P(dom, "cuts", None, None, None),
        ),
        out_specs=P((*dom, "cuts"), None),
        check_vma=False,
    )
```

```python
import jax
import jax.numpy as jnp
from jax import lax
from jax.experimental import pallas as pl
from jax.experimental.pallas import tpu as pltpu
from jax.sharding import PartitionSpec as P

ROWS = 384
SLOT = 16
HUB = 16
BLOCK = 128
CHUNK = 16
CORES = 2
DEAD = 2.0**100
DEAD_LIMIT = 2.0**50
VMEM = pltpu.VMEM
SMEM = pltpu.SMEM
F32 = jnp.float32
BF16 = jnp.bfloat16


def spec(space):
    return pl.BlockSpec(memory_space=space)


LIMIT = 40 * 1024 * 1024


def call(body, out_shape, spaces, scratch=(), cost=None):
    return pl.pallas_call(
        body,
        out_shape=out_shape,
        in_specs=[spec(s) for s in spaces],
        out_specs=jax.tree.map(lambda _: spec(VMEM), out_shape),
        scratch_shapes=list(scratch),
        cost_estimate=cost,
        compiler_params=pltpu.CompilerParams(vmem_limit_bytes=LIMIT),
    )


def column(row, size):
    here = lax.broadcasted_iota(jnp.int32, (size, size), 0)
    there = lax.broadcasted_iota(jnp.int32, (size, size), 1)
    return jnp.sum(jnp.where(here == there, row, 0), axis=1, keepdims=True)


def one_hot(picks):
    places = lax.broadcasted_iota(jnp.int32, picks.shape, 1)
    return jnp.where(picks == places, 1.0, 0.0).astype(BF16)


def fill_outgoing(table, picks, hub_picks, out, dead):
    parts, slots = picks.shape
    width = table.shape[1]
    hubs = jnp.dot(one_hot(hub_picks), table, preferred_element_type=F32).astype(BF16)
    for first in range(0, parts, CHUNK):
        some = picks[first : first + CHUNK]
        wide = jnp.broadcast_to(some[:, :, None], (CHUNK, slots, ROWS)).reshape(
            CHUNK * slots, ROWS
        )
        rows = jnp.dot(one_hot(wide), table, preferred_element_type=F32)
        if dead != 0.0:
            rows = jnp.where(wide[:, :width] < 0, dead, rows)
        chips = pl.ds(first // CORES, CHUNK // CORES)
        pairs = rows.astype(BF16).reshape(CHUNK // CORES, CORES, slots, width)
        core = lax.axis_index("core")
        out[chips, :slots] = jnp.where(core == 0, pairs[:, 0], pairs[:, 1])
        out[chips, slots : CORES * slots] = jnp.where(core == 0, pairs[:, 1], pairs[:, 0])
        out[chips, CORES * slots :] = jnp.broadcast_to(
            hubs[None], (CHUNK // CORES,) + hubs.shape
        )


def slots_body(out):
    out[...] = lax.broadcasted_iota(jnp.int32, out.shape, 0)


def slot_numbers(slots, parts):
    return call(
        slots_body,
        jax.ShapeDtypeStruct((slots, parts), jnp.int32),
        [],
        cost=pl.CostEstimate(flops=10**9, bytes_accessed=4 * 10**6, transcendentals=0),
    )()


def pack_body(*refs):
    count = (len(refs) - 3 - 5) // 2
    handed, (slot, halo_rows, halo_count, hub_rows, table) = refs[:count], refs[count : count + 5]
    out, picks_out, hubs_out, *handed_out = refs[count + 5 :]
    picks = jnp.where(slot[...] < halo_count[...], halo_rows[...], -1).T
    hub_picks = jnp.broadcast_to(column(hub_rows[...], HUB), (HUB, ROWS))
    picks_out[...] = picks
    hubs_out[...] = hub_picks
    fill_outgoing(table[...], picks, hub_picks, out, 0.0)
    for source, place in zip(handed, handed_out, strict=True):
        place[...] = source[...]


def pack(handed, halo_rows, halo_count, hub_rows, table):
    slots, parts = halo_rows.shape
    operands = (slot_numbers(slots, parts), halo_rows, halo_count, hub_rows, table)
    return call(
        pack_body,
        (
            jax.ShapeDtypeStruct(
                (parts // CORES, CORES * SLOT + HUB, table.shape[1]), BF16
            ),
            jax.ShapeDtypeStruct((parts, slots), jnp.int32),
            jax.ShapeDtypeStruct((HUB, ROWS), jnp.int32),
            *(jax.ShapeDtypeStruct(x.shape, x.dtype) for x in handed),
        ),
        [VMEM] * (len(handed) + len(operands)),
    )(*handed, *operands)


def plan_body(targets, columns, used, out):
    capacity = targets.shape[1]
    out[...] = jnp.broadcast_to(used[...], out.shape)
    out[:, :capacity] = targets[...]
    out[:, capacity : 2 * capacity] = columns[...]


def tile_plan(targets, columns, used):
    return call(
        plan_body, jax.ShapeDtypeStruct((1, 128), jnp.int32), [VMEM] * 3
    )(targets, columns, used)


def sum_body(plan, own, received, passed, tiles, *rest):
    *layer, out, mine, total = rest
    total[...] = jnp.zeros_like(total)
    capacity = tiles.shape[0]
    group = BLOCK // (CORES * SLOT)
    groups = received.shape[0] // group
    core = lax.axis_index("core")
    own_blocks = ROWS // BLOCK
    used = plan[2 * capacity]
    for i in range(capacity):
        col = plan[capacity + i]
        here = jnp.minimum(col, own_blocks - 1)
        local_rows = own[pl.ds(pl.multiple_of(here * BLOCK, BLOCK), BLOCK), :]
        away = jnp.maximum(col - own_blocks, 0)
        hub = jnp.where(away >= groups, 1, 0)
        first = pl.multiple_of((away - hub * groups) * group, group)
        start = pl.multiple_of(hub * SLOT, SLOT)
        same = received[pl.ds(first, group), pl.ds(pl.multiple_of(start * CORES, SLOT), SLOT), :]
        other = passed[pl.ds(first, group), pl.ds(start, SLOT), :]
        remote_rows = jnp.stack(
            [jnp.where(core == 0, same, other), jnp.where(core == 0, other, same)],
            axis=1,
        ).reshape(BLOCK, own.shape[1])
        rows = jnp.where(col < own_blocks, local_rows, remote_rows)
        if layer:
            weight, bias = layer
            hidden = jnp.dot(rows, weight[...], preferred_element_type=F32)
            hidden = jnp.maximum(hidden + bias[...], 0.0)
            live = rows.astype(F32) < DEAD_LIMIT
            live = jnp.concatenate([live] * (hidden.shape[1] // live.shape[1]), axis=1)
            rows = jnp.where(live, hidden, 0.0).astype(BF16)
        term = jnp.dot(tiles[i], rows, preferred_element_type=F32)
        row = plan[i]
        total[row] = total[row] + jnp.where(i < used, term, 0.0)
    chunk = ROWS // BLOCK
    cut = lax.axis_index("cuts")
    mine[...] = total[pl.ds(cut * chunk, chunk)].reshape(mine.shape)
    out[...] = total[...].astype(BF16).reshape(out.shape)


def tile_sums(own, received, passed, plan, tiles, cuts, *layer):
    width = layer[0].shape[1] if layer else own.shape[1]
    return call(
        sum_body,
        (
            jax.ShapeDtypeStruct((cuts, ROWS, width), BF16),
            jax.ShapeDtypeStruct((ROWS, width), F32),
        ),
        [SMEM] + [VMEM] * (4 + len(layer)),
        [pltpu.VMEM((cuts * ROWS // BLOCK, BLOCK, width), F32)],
    )(plan, own, received, passed, tiles, *layer)


def over_cuts(parts, mine):
    cut = lax.axis_index("cuts")
    total = mine[...]
    for k in range(parts.shape[0]):
        total = total + jnp.where(cut == k, 0.0, parts[k].astype(F32))
    return total


def middle_body(parts, mine, picks, hub_picks, table, out):
    rows = over_cuts(parts, mine).astype(BF16)
    table[...] = rows
    fill_outgoing(rows, picks[...], hub_picks[...], out, DEAD)


def middle(parts, mine, picks, hub_picks):
    width = mine.shape[1]
    return call(
        middle_body,
        (
            jax.ShapeDtypeStruct((ROWS, width), BF16),
            jax.ShapeDtypeStruct((picks.shape[0] // CORES, CORES * SLOT + HUB, width), BF16),
        ),
        [VMEM] * 4,
    )(parts, mine, picks, hub_picks)


def last_body(parts, mine, weight, bias, out):
    total = over_cuts(parts, mine)
    high = total.astype(BF16)
    low = (total - high.astype(F32)).astype(BF16)
    hidden = jnp.dot(high, weight[...], preferred_element_type=F32) + jnp.dot(
        low, weight[...], preferred_element_type=F32
    )
    out[...] = jnp.maximum(hidden + bias[...], 0.0).astype(BF16)


def swap(rows, axis):
    return lax.all_to_all(rows, axis, split_axis=0, concat_axis=0, tiled=True)


def exchange(rows):
    received = swap(rows, "chip")
    return received, lax.ppermute(received[:, SLOT:], "core", [(0, 1), (1, 0)])


def local(
    features,
    weight_one,
    bias_one,
    weight_two,
    bias_two,
    hub_rows,
    halo_rows,
    halo_count,
    tile_target,
    tile_source,
    tile_count,
    tile_values,
):
    cuts = lax.axis_size("cuts")
    halo_rows = halo_rows.reshape(halo_rows.shape[2:]).T
    tiles = tile_values.reshape(tile_values.shape[2:])
    row = lambda x: x.reshape(1, -1)
    outgoing, picks, hub_picks, bias_one, bias_two = pack(
        (row(bias_one), row(bias_two)),
        halo_rows,
        row(halo_count),
        row(hub_rows),
        features,
    )
    plan = tile_plan(row(tile_target), row(tile_source), row(tile_count)).reshape(-1)
    parts, mine = tile_sums(features, *exchange(outgoing), plan, tiles, cuts)
    table, outgoing = middle(swap(parts, "cuts"), mine, picks, hub_picks)
    parts, mine = tile_sums(
        table, *exchange(outgoing), plan, tiles, cuts, weight_one, bias_one
    )
    return call(
        last_body,
        jax.ShapeDtypeStruct((ROWS, weight_two.shape[1]), BF16),
        [VMEM] * 4,
    )(swap(parts, "cuts"), mine, weight_two, bias_two)


def solution(mesh):
    cuts = mesh.shape["cuts"]
    chips = jax.sharding.Mesh(
        mesh.devices.reshape(-1, CORES, cuts), ("chip", "core", "cuts")
    )
    dom = ("chip", "core")
    return jax.shard_map(
        local,
        mesh=chips,
        in_specs=(
            P((*dom, "cuts"), None),
            P(),
            P(),
            P(),
            P(),
            P(dom, "cuts", None),
            P(dom, "cuts", None, None),
            P(dom, "cuts", None),
            P(dom, "cuts", None),
            P(dom, "cuts", None),
            P(dom, "cuts"),
            P(dom, "cuts", None, None, None),
        ),
        out_specs=P((*dom, "cuts"), None),
        check_vma=False,
    )
```

```python
import functools

import jax
import jax.numpy as jnp
from jax import lax
from jax.experimental import pallas as pl
from jax.experimental.pallas import tpu as pltpu
from jax.sharding import PartitionSpec as P

ROWS = 384
SLOT = 16
HUB = 16
BLOCK = 128
CHUNK = 16
CORES = 2
HIDDEN_ROWS = 512
DEAD = 2.0**100
DEAD_LIMIT = 2.0**50
VMEM = pltpu.VMEM
SMEM = pltpu.SMEM
F32 = jnp.float32
BF16 = jnp.bfloat16


def spec(space):
    return pl.BlockSpec(memory_space=space)


LIMIT = 40 * 1024 * 1024


def call(body, out_shape, spaces, scratch=(), cost=None):
    return pl.pallas_call(
        body,
        out_shape=out_shape,
        in_specs=[spec(s) for s in spaces],
        out_specs=jax.tree.map(lambda _: spec(VMEM), out_shape),
        scratch_shapes=list(scratch),
        cost_estimate=cost,
        compiler_params=pltpu.CompilerParams(vmem_limit_bytes=LIMIT),
    )


def column(row, size):
    here = lax.broadcasted_iota(jnp.int32, (size, size), 0)
    there = lax.broadcasted_iota(jnp.int32, (size, size), 1)
    return jnp.sum(jnp.where(here == there, row, 0), axis=1, keepdims=True)


def one_hot(picks):
    places = lax.broadcasted_iota(jnp.int32, picks.shape, 1)
    return jnp.where(picks == places, 1.0, 0.0).astype(BF16)


def fill_outgoing(table, picks, hub_picks, out, dead):
    parts, slots = picks.shape
    width = table.shape[1]
    hubs = jnp.dot(one_hot(hub_picks), table, preferred_element_type=F32).astype(BF16)
    for first in range(0, parts, CHUNK):
        some = picks[first : first + CHUNK]
        wide = jnp.broadcast_to(some[:, :, None], (CHUNK, slots, ROWS)).reshape(
            CHUNK * slots, ROWS
        )
        rows = jnp.dot(one_hot(wide), table, preferred_element_type=F32)
        if dead != 0.0:
            rows = jnp.where(wide[:, :width] < 0, dead, rows)
        chips = pl.ds(first // CORES, CHUNK // CORES)
        pairs = rows.astype(BF16).reshape(CHUNK // CORES, CORES, slots, width)
        core = lax.axis_index("core")
        out[chips, :slots] = jnp.where(core == 0, pairs[:, 0], pairs[:, 1])
        out[chips, slots : CORES * slots] = jnp.where(core == 0, pairs[:, 1], pairs[:, 0])
        out[chips, CORES * slots :] = jnp.broadcast_to(
            hubs[None], (CHUNK // CORES,) + hubs.shape
        )


def slots_body(out):
    out[...] = lax.broadcasted_iota(jnp.int32, out.shape, 0)


def slot_numbers(slots, parts):
    return call(
        slots_body,
        jax.ShapeDtypeStruct((slots, parts), jnp.int32),
        [],
        cost=pl.CostEstimate(flops=10**9, bytes_accessed=4 * 10**6, transcendentals=0),
    )()


def pack_body(*refs):
    count = (len(refs) - 3 - 5) // 2
    handed, (slot, halo_rows, halo_count, hub_rows, table) = refs[:count], refs[count : count + 5]
    out, picks_out, hubs_out, *handed_out = refs[count + 5 :]
    picks = jnp.where(slot[...] < halo_count[...], halo_rows[...], -1).T
    hub_picks = jnp.broadcast_to(column(hub_rows[...], HUB), (HUB, ROWS))
    picks_out[...] = picks
    hubs_out[...] = hub_picks
    fill_outgoing(table[...], picks, hub_picks, out, 0.0)
    for source, place in zip(handed, handed_out, strict=True):
        place[...] = source[...]


def pack(handed, halo_rows, halo_count, hub_rows, table):
    slots, parts = halo_rows.shape
    operands = (slot_numbers(slots, parts), halo_rows, halo_count, hub_rows, table)
    return call(
        pack_body,
        (
            jax.ShapeDtypeStruct(
                (parts // CORES, CORES * SLOT + HUB, table.shape[1]), BF16
            ),
            jax.ShapeDtypeStruct((parts, slots), jnp.int32),
            jax.ShapeDtypeStruct((HUB, ROWS), jnp.int32),
            *(jax.ShapeDtypeStruct(x.shape, x.dtype) for x in handed),
        ),
        [VMEM] * (len(handed) + len(operands)),
    )(*handed, *operands)


def plan_body(targets, columns, used, out):
    capacity = targets.shape[1]
    out[...] = jnp.broadcast_to(used[...], out.shape)
    out[:, :capacity] = targets[...]
    out[:, capacity : 2 * capacity] = columns[...]


def tile_plan(targets, columns, used):
    return call(
        plan_body, jax.ShapeDtypeStruct((1, 128), jnp.int32), [VMEM] * 3
    )(targets, columns, used)


def sum_body(layers, plan, own, received, passed, tiles, *rest):
    layer, (out, mine, total, *scratch) = rest[:layers], rest[layers:]
    total[...] = jnp.zeros_like(total)
    capacity = tiles.shape[0]
    group = BLOCK // (CORES * SLOT)
    groups = received.shape[0] // group
    core = lax.axis_index("core")
    own_blocks = ROWS // BLOCK
    used = plan[2 * capacity]

    def source_rows(i):
        col = plan[capacity + i]
        here = jnp.minimum(col, own_blocks - 1)
        local_rows = own[pl.ds(pl.multiple_of(here * BLOCK, BLOCK), BLOCK), :]
        away = jnp.maximum(col - own_blocks, 0)
        hub = jnp.where(away >= groups, 1, 0)
        first = pl.multiple_of((away - hub * groups) * group, group)
        start = pl.multiple_of(hub * SLOT, SLOT)
        same = received[pl.ds(first, group), pl.ds(pl.multiple_of(start * CORES, SLOT), SLOT), :]
        other = passed[pl.ds(first, group), pl.ds(start, SLOT), :]
        remote_rows = jnp.stack(
            [jnp.where(core == 0, same, other), jnp.where(core == 0, other, same)],
            axis=1,
        ).reshape(BLOCK, own.shape[1])
        return jnp.where(col < own_blocks, local_rows, remote_rows)

    if layer:
        (weight, bias), (picked, values) = layer, scratch
        for i in range(capacity):
            picked[i * BLOCK : (i + 1) * BLOCK] = source_rows(i)
        for first in range(0, capacity * BLOCK, HIDDEN_ROWS):
            span = pl.ds(first, HIDDEN_ROWS)
            rows = picked[span]
            hidden = jnp.dot(rows, weight[...], preferred_element_type=F32)
            hidden = jnp.maximum(hidden + bias[...], 0.0)
            live = rows.astype(F32) < DEAD_LIMIT
            live = jnp.concatenate([live] * (hidden.shape[1] // live.shape[1]), axis=1)
            values[span] = jnp.where(live, hidden, 0.0).astype(BF16)
    for i in range(capacity):
        rows = values[i * BLOCK : (i + 1) * BLOCK] if layer else source_rows(i)
        term = jnp.dot(tiles[i], rows, preferred_element_type=F32)
        row = plan[i]
        total[row] = total[row] + jnp.where(i < used, term, 0.0)
    chunk = ROWS // BLOCK
    cut = lax.axis_index("cuts")
    mine[...] = total[pl.ds(cut * chunk, chunk)].reshape(mine.shape)
    out[...] = total[...].astype(BF16).reshape(out.shape)


def tile_sums(own, received, passed, plan, tiles, cuts, *layer):
    width = layer[0].shape[1] if layer else own.shape[1]
    rows = tiles.shape[0] * BLOCK
    scratch = [pltpu.VMEM((cuts * ROWS // BLOCK, BLOCK, width), F32)]
    if layer:
        scratch += [pltpu.VMEM((rows, own.shape[1]), BF16), pltpu.VMEM((rows, width), BF16)]
    return call(
        functools.partial(sum_body, len(layer)),
        (
            jax.ShapeDtypeStruct((cuts, ROWS, width), BF16),
            jax.ShapeDtypeStruct((ROWS, width), F32),
        ),
        [SMEM] + [VMEM] * (4 + len(layer)),
        scratch,
    )(plan, own, received, passed, tiles, *layer)


def over_cuts(parts, mine):
    cut = lax.axis_index("cuts")
    total = mine[...]
    for k in range(parts.shape[0]):
        total = total + jnp.where(cut == k, 0.0, parts[k].astype(F32))
    return total


def middle_body(parts, mine, picks, hub_picks, table, out):
    rows = over_cuts(parts, mine).astype(BF16)
    table[...] = rows
    fill_outgoing(rows, picks[...], hub_picks[...], out, DEAD)


def middle(parts, mine, picks, hub_picks):
    width = mine.shape[1]
    return call(
        middle_body,
        (
            jax.ShapeDtypeStruct((ROWS, width), BF16),
            jax.ShapeDtypeStruct((picks.shape[0] // CORES, CORES * SLOT + HUB, width), BF16),
        ),
        [VMEM] * 4,
    )(parts, mine, picks, hub_picks)


def last_body(parts, mine, weight, bias, out):
    total = over_cuts(parts, mine)
    high = total.astype(BF16)
    low = (total - high.astype(F32)).astype(BF16)
    hidden = jnp.dot(high, weight[...], preferred_element_type=F32) + jnp.dot(
        low, weight[...], preferred_element_type=F32
    )
    out[...] = jnp.maximum(hidden + bias[...], 0.0).astype(BF16)


def swap(rows, axis):
    return lax.all_to_all(rows, axis, split_axis=0, concat_axis=0, tiled=True)


def exchange(rows):
    received = swap(rows, "chip")
    return received, lax.ppermute(received[:, SLOT:], "core", [(0, 1), (1, 0)])


def local(
    features,
    weight_one,
    bias_one,
    weight_two,
    bias_two,
    hub_rows,
    halo_rows,
    halo_count,
    tile_target,
    tile_source,
    tile_count,
    tile_values,
):
    cuts = lax.axis_size("cuts")
    halo_rows = halo_rows.reshape(halo_rows.shape[2:]).T
    tiles = tile_values.reshape(tile_values.shape[2:])
    row = lambda x: x.reshape(1, -1)
    outgoing, picks, hub_picks, bias_one, bias_two = pack(
        (row(bias_one), row(bias_two)),
        halo_rows,
        row(halo_count),
        row(hub_rows),
        features,
    )
    plan = tile_plan(row(tile_target), row(tile_source), row(tile_count)).reshape(-1)
    parts, mine = tile_sums(features, *exchange(outgoing), plan, tiles, cuts)
    table, outgoing = middle(swap(parts, "cuts"), mine, picks, hub_picks)
    parts, mine = tile_sums(
        table, *exchange(outgoing), plan, tiles, cuts, weight_one, bias_one
    )
    return call(
        last_body,
        jax.ShapeDtypeStruct((ROWS, weight_two.shape[1]), BF16),
        [VMEM] * 4,
    )(swap(parts, "cuts"), mine, weight_two, bias_two)


def solution(mesh):
    cuts = mesh.shape["cuts"]
    chips = jax.sharding.Mesh(
        mesh.devices.reshape(-1, CORES, cuts), ("chip", "core", "cuts")
    )
    dom = ("chip", "core")
    return jax.shard_map(
        local,
        mesh=chips,
        in_specs=(
            P((*dom, "cuts"), None),
            P(),
            P(),
            P(),
            P(),
            P(dom, "cuts", None),
            P(dom, "cuts", None, None),
            P(dom, "cuts", None),
            P(dom, "cuts", None),
            P(dom, "cuts", None),
            P(dom, "cuts"),
            P(dom, "cuts", None, None, None),
        ),
        out_specs=P((*dom, "cuts"), None),
        check_vma=False,
    )
```

```python
import jax
import jax.numpy as jnp
from jax import lax
from jax.experimental import pallas as pl
from jax.experimental.pallas import tpu as pltpu
from jax.sharding import PartitionSpec as P

ROWS = 384
SLOT = 16
HUB = 16
BLOCK = 128
CHUNK = 16
CORES = 2
DEAD = 2.0**100
DEAD_LIMIT = 2.0**50
VMEM = pltpu.VMEM
SMEM = pltpu.SMEM
F32 = jnp.float32
BF16 = jnp.bfloat16


def spec(space):
    return pl.BlockSpec(memory_space=space)


LIMIT = 40 * 1024 * 1024


def call(body, out_shape, spaces, scratch=(), cost=None):
    return pl.pallas_call(
        body,
        out_shape=out_shape,
        in_specs=[spec(s) for s in spaces],
        out_specs=jax.tree.map(lambda _: spec(VMEM), out_shape),
        scratch_shapes=list(scratch),
        cost_estimate=cost,
        compiler_params=pltpu.CompilerParams(vmem_limit_bytes=LIMIT),
    )


def column(row, size):
    here = lax.broadcasted_iota(jnp.int32, (size, size), 0)
    there = lax.broadcasted_iota(jnp.int32, (size, size), 1)
    return jnp.sum(jnp.where(here == there, row, 0), axis=1, keepdims=True)


def one_hot(picks):
    places = lax.broadcasted_iota(jnp.int32, picks.shape, 1)
    return jnp.where(picks == places, 1.0, 0.0).astype(BF16)


def fill_outgoing(table, picks, hub_picks, out, dead):
    parts, slots = picks.shape
    width = table.shape[1]
    hubs = jnp.dot(one_hot(hub_picks), table, preferred_element_type=F32).astype(BF16)
    for first in range(0, parts, CHUNK):
        some = picks[first : first + CHUNK]
        wide = jnp.broadcast_to(some[:, :, None], (CHUNK, slots, ROWS)).reshape(
            CHUNK * slots, ROWS
        )
        rows = jnp.dot(one_hot(wide), table, preferred_element_type=F32)
        if dead != 0.0:
            rows = jnp.where(wide[:, :width] < 0, dead, rows)
        chips = pl.ds(first // CORES, CHUNK // CORES)
        pairs = rows.astype(BF16).reshape(CHUNK // CORES, CORES, slots, width)
        core = lax.axis_index("core")
        out[chips, :slots] = jnp.where(core == 0, pairs[:, 0], pairs[:, 1])
        out[chips, slots : CORES * slots] = jnp.where(core == 0, pairs[:, 1], pairs[:, 0])
        out[chips, CORES * slots :] = jnp.broadcast_to(
            hubs[None], (CHUNK // CORES,) + hubs.shape
        )


def slots_body(out):
    out[...] = lax.broadcasted_iota(jnp.int32, out.shape, 0)


def slot_numbers(slots, parts):
    return call(
        slots_body,
        jax.ShapeDtypeStruct((slots, parts), jnp.int32),
        [],
        cost=pl.CostEstimate(flops=10**9, bytes_accessed=4 * 10**6, transcendentals=0),
    )()


def pack_body(*refs):
    count = (len(refs) - 3 - 5) // 2
    handed, (slot, halo_rows, halo_count, hub_rows, table) = refs[:count], refs[count : count + 5]
    out, picks_out, hubs_out, *handed_out = refs[count + 5 :]
    picks = jnp.where(slot[...] < halo_count[...], halo_rows[...], -1).T
    hub_picks = jnp.broadcast_to(column(hub_rows[...], HUB), (HUB, ROWS))
    picks_out[...] = picks
    hubs_out[...] = hub_picks
    fill_outgoing(table[...], picks, hub_picks, out, 0.0)
    for source, place in zip(handed, handed_out, strict=True):
        place[...] = source[...]


def pack(handed, halo_rows, halo_count, hub_rows, table):
    slots, parts = halo_rows.shape
    operands = (slot_numbers(slots, parts), halo_rows, halo_count, hub_rows, table)
    return call(
        pack_body,
        (
            jax.ShapeDtypeStruct(
                (parts // CORES, CORES * SLOT + HUB, table.shape[1]), BF16
            ),
            jax.ShapeDtypeStruct((parts, slots), jnp.int32),
            jax.ShapeDtypeStruct((HUB, ROWS), jnp.int32),
            *(jax.ShapeDtypeStruct(x.shape, x.dtype) for x in handed),
        ),
        [VMEM] * (len(handed) + len(operands)),
    )(*handed, *operands)


def plan_body(targets, columns, used, first, second, out, first_out, second_out):
    capacity = targets.shape[1]
    out[...] = jnp.broadcast_to(used[...], out.shape)
    out[:, :capacity] = targets[...]
    out[:, capacity : 2 * capacity] = columns[...]
    first_out[...] = first[...]
    second_out[...] = second[...]


def tile_plan(targets, columns, used, *biases):
    return call(
        plan_body,
        (
            jax.ShapeDtypeStruct((1, 128), jnp.int32),
            *(jax.ShapeDtypeStruct(x.shape, x.dtype) for x in biases),
        ),
        [VMEM] * 5,
    )(targets, columns, used, *biases)


def sum_body(plan, own, received, passed, tiles, *rest):
    *layer, out, mine, total = rest
    total[...] = jnp.zeros_like(total)
    capacity = tiles.shape[0]
    group = BLOCK // (CORES * SLOT)
    groups = received.shape[0] // group
    core = lax.axis_index("core")
    own_blocks = ROWS // BLOCK
    used = plan[2 * capacity]
    for i in range(capacity):
        col = plan[capacity + i]
        here = jnp.minimum(col, own_blocks - 1)
        local_rows = own[pl.ds(pl.multiple_of(here * BLOCK, BLOCK), BLOCK), :]
        away = jnp.maximum(col - own_blocks, 0)
        hub = jnp.where(away >= groups, 1, 0)
        first = pl.multiple_of((away - hub * groups) * group, group)
        start = pl.multiple_of(hub * SLOT, SLOT)
        same = received[pl.ds(first, group), pl.ds(pl.multiple_of(start * CORES, SLOT), SLOT), :]
        other = passed[pl.ds(first, group), pl.ds(start, SLOT), :]
        remote_rows = jnp.stack(
            [jnp.where(core == 0, same, other), jnp.where(core == 0, other, same)],
            axis=1,
        ).reshape(BLOCK, own.shape[1])
        rows = jnp.where(col < own_blocks, local_rows, remote_rows)
        if layer:
            weight, bias = layer
            hidden = jnp.dot(rows, weight[...], preferred_element_type=F32)
            hidden = jnp.maximum(hidden + bias[...], 0.0)
            live = rows.astype(F32) < DEAD_LIMIT
            live = jnp.concatenate([live] * (hidden.shape[1] // live.shape[1]), axis=1)
            rows = jnp.where(live, hidden, 0.0).astype(BF16)
        term = jnp.dot(tiles[i], rows, preferred_element_type=F32)
        row = plan[i]
        total[row] = total[row] + jnp.where(i < used, term, 0.0)
    chunk = ROWS // BLOCK
    cut = lax.axis_index("cuts")
    mine[...] = total[pl.ds(cut * chunk, chunk)].reshape(mine.shape)
    out[...] = total[...].astype(BF16).reshape(out.shape)


def tile_sums(own, received, passed, plan, tiles, cuts, *layer):
    width = layer[0].shape[1] if layer else own.shape[1]
    return call(
        sum_body,
        (
            jax.ShapeDtypeStruct((cuts, ROWS, width), BF16),
            jax.ShapeDtypeStruct((ROWS, width), F32),
        ),
        [SMEM] + [VMEM] * (4 + len(layer)),
        [pltpu.VMEM((cuts * ROWS // BLOCK, BLOCK, width), F32)],
    )(plan, own, received, passed, tiles, *layer)


def over_cuts(parts, mine):
    cut = lax.axis_index("cuts")
    total = mine[...]
    for k in range(parts.shape[0]):
        total = total + jnp.where(cut == k, 0.0, parts[k].astype(F32))
    return total


def middle_body(parts, mine, picks, hub_picks, table, out):
    rows = over_cuts(parts, mine).astype(BF16)
    table[...] = rows
    fill_outgoing(rows, picks[...], hub_picks[...], out, DEAD)


def middle(parts, mine, picks, hub_picks):
    width = mine.shape[1]
    return call(
        middle_body,
        (
            jax.ShapeDtypeStruct((ROWS, width), BF16),
            jax.ShapeDtypeStruct((picks.shape[0] // CORES, CORES * SLOT + HUB, width), BF16),
        ),
        [VMEM] * 4,
    )(parts, mine, picks, hub_picks)


def last_body(parts, mine, weight, bias, out):
    total = over_cuts(parts, mine)
    high = total.astype(BF16)
    low = (total - high.astype(F32)).astype(BF16)
    hidden = jnp.dot(high, weight[...], preferred_element_type=F32) + jnp.dot(
        low, weight[...], preferred_element_type=F32
    )
    out[...] = jnp.maximum(hidden + bias[...], 0.0).astype(BF16)


def swap(rows, axis):
    return lax.all_to_all(rows, axis, split_axis=0, concat_axis=0, tiled=True)


def exchange(rows):
    received = swap(rows, "chip")
    return received, lax.ppermute(received[:, SLOT:], "core", [(0, 1), (1, 0)])


def local(
    features,
    weight_one,
    bias_one,
    weight_two,
    bias_two,
    hub_rows,
    halo_rows,
    halo_count,
    tile_target,
    tile_source,
    tile_count,
    tile_values,
):
    cuts = lax.axis_size("cuts")
    halo_rows = halo_rows.reshape(halo_rows.shape[2:]).T
    tiles = tile_values.reshape(tile_values.shape[2:])
    row = lambda x: x.reshape(1, -1)
    outgoing, picks, hub_picks = pack(
        (), halo_rows, row(halo_count), row(hub_rows), features
    )
    plan, bias_one, bias_two = tile_plan(
        row(tile_target), row(tile_source), row(tile_count), row(bias_one), row(bias_two)
    )
    plan = plan.reshape(-1)
    parts, mine = tile_sums(features, *exchange(outgoing), plan, tiles, cuts)
    table, outgoing = middle(swap(parts, "cuts"), mine, picks, hub_picks)
    parts, mine = tile_sums(
        table, *exchange(outgoing), plan, tiles, cuts, weight_one, bias_one
    )
    return call(
        last_body,
        jax.ShapeDtypeStruct((ROWS, weight_two.shape[1]), BF16),
        [VMEM] * 4,
    )(swap(parts, "cuts"), mine, weight_two, bias_two)


def solution(mesh):
    cuts = mesh.shape["cuts"]
    chips = jax.sharding.Mesh(
        mesh.devices.reshape(-1, CORES, cuts), ("chip", "core", "cuts")
    )
    dom = ("chip", "core")
    return jax.shard_map(
        local,
        mesh=chips,
        in_specs=(
            P((*dom, "cuts"), None),
            P(),
            P(),
            P(),
            P(),
            P(dom, "cuts", None),
            P(dom, "cuts", None, None),
            P(dom, "cuts", None),
            P(dom, "cuts", None),
            P(dom, "cuts", None),
            P(dom, "cuts"),
            P(dom, "cuts", None, None, None),
        ),
        out_specs=P((*dom, "cuts"), None),
        check_vma=False,
    )
```
